32 devices in a mesh: sky: 4 (over y, x), tm: 4 (over z), fov: 2 (over core).
Axes of the slice: x: 2, y: 2, z: 4, core: 2. Of those that a mesh axis runs over, the one named last changes fastest.
Arguments:
- src_partials: float32 [65536, 5, 128], P(('sky', 'tm', 'fov')), may hold values from -0.375 to 0.375
- att_partials: float32 [65536, 4, 128], P(('sky', 'tm', 'fov')), may hold values from -0.3 to 0.3
- cal_partials: float32 [65536, 128], P(('sky', 'tm', 'fov')), may hold values from -0.6 to 0.6
- obs_phase: float32 [65536, 128], P(('sky', 'tm', 'fov')), may hold values from 0 to 1
- obs_residual: float32 [65536, 128], P(('sky', 'tm', 'fov')), may hold values from -6 to 6
- block_source: int32 [65536], P(('sky', 'tm', 'fov')), may hold values from 0 to 4095
- block_segment: int32 [65536], P(('sky', 'tm', 'fov')), may hold values from 0 to 511, as said below
- block_unit: int32 [65536], P(('sky', 'tm', 'fov')), may hold values from 0 to 524287, as said below
- live_blocks: int32 [32], P(('sky', 'tm', 'fov')), may hold values from 896 to 2048, as said below
Outputs:
- src_update: float32 [5, 16384], P(None, 'sky')
- att_update: float32 [4, 4, 512], P(None, 'tm', 'sky')
- cal_update: float32 [524288], P(('sky', 'tm', 'fov'))
The draws below stay inside these ranges and needn't reach their ends.
Inputs may be any that keep to these rules, and one draw needn't show every extreme that they name: `block_segment`: only live blocks' segments matter. Of one device's live blocks at most 512 have segments of one sky index (s * 128 to (s + 1) * 128 - 1); for every tm and fov index some sky index s has exactly 512 such live blocks from every device of that tm and fov index. A device's live blocks are its first live_blocks blocks. `block_unit`: units fall into 32 ranges of 524288 / 32 units each (range r is the units of output shard r). Of one device's blocks, live or not, at most 128 have units of one range; on every device some range has exactly 128.
All inputs are finite; a program needn't handle non-finite values.
Results may differ from the reference program's by a relative error of at most 0.00011.
Values sent between devices are 32-bit elements; how exact they have to be, the bound alone decides.
A program may use at most 128 MiB of HBM per device.

```python
import jax
import jax.numpy as jnp
from jax import lax

SRC_DEV = 4096
BLK_DEV = 2048
SEG_DEV = 128
OBS = 128
CAL = 524288
SRC = 16384
BLOCKS = 65536
SEG_ARC = 512
N_SKY = 4
N_TM = 4
N_FOV = 2


def block_layout(key):
    key = jax.random.fold_in(key, 7)
    key_count, key_hot, key_segment, key_order = jax.random.split(key, 4)
    capacity = BLK_DEV // N_SKY
    device_total = N_SKY * N_TM * N_FOV
    counts = jax.random.randint(key_count, (N_SKY, N_TM, N_FOV, N_SKY), capacity // 4, capacity + 1)
    hottest = jax.random.randint(key_hot, (1, N_TM, N_FOV, 1), 0, N_SKY)
    column = jnp.arange(N_SKY).reshape(1, 1, 1, N_SKY)
    counts = jnp.where(column == hottest, capacity, counts)
    counts = counts.at[0, 0, 0, :].set(capacity)
    lowest = jnp.where(jnp.arange(N_SKY) == hottest[0, N_TM - 1, N_FOV - 1, 0], capacity, capacity // 4)
    counts = counts.at[N_SKY - 1, N_TM - 1, N_FOV - 1, :].set(lowest)
    counts = counts.reshape(device_total, N_SKY)
    slots = jnp.arange(BLK_DEV, dtype=jnp.int32)
    target = slots // capacity
    ranks = slots % capacity
    live_slot = (ranks[None, :] < jnp.take(counts, target, axis=1)).astype(jnp.int32)
    within = jax.random.randint(key_segment, (device_total, BLK_DEV), 0, SEG_DEV)
    segment = target[None, :] * SEG_DEV + within
    scores = jax.random.randint(key_order, (device_total, BLK_DEV), 0, BLK_DEV) * BLK_DEV + slots[None, :]
    first = jnp.argsort(scores, axis=1)
    live_sorted = jnp.take_along_axis(live_slot, first, axis=1)
    second = jnp.argsort(1 - live_sorted, axis=1, stable=True)
    order = jnp.take_along_axis(first, second, axis=1)
    segment = jnp.take_along_axis(segment, order, axis=1).reshape(-1)
    totals = jnp.sum(live_slot, axis=1)
    return (segment.astype(jnp.int32), totals.astype(jnp.int32))


def draw_block_segment(key, part):
    return block_layout(key)[0]


def draw_live_blocks(key, part):
    return block_layout(key)[1]


def unit_row(key):
    key_hot, key_order, key_shuffle, key_unit = jax.random.split(key, 4)
    owners = N_SKY * N_TM * N_FOV
    ucap = max(2, 2 * BLK_DEV // owners)
    share = CAL // owners
    slot_total = owners * ucap
    slots = jnp.arange(slot_total, dtype=jnp.int32)
    hot = jax.random.randint(key_hot, (), 0, owners)
    scores = jax.random.randint(key_order, (slot_total,), 0, slot_total) * slot_total + slots
    scores = jnp.where(slots // ucap == hot, slots - slot_total, scores)
    chosen = jnp.argsort(scores)[:BLK_DEV]
    chosen = jax.random.permutation(key_shuffle, chosen)
    owner = chosen // ucap
    inner = jax.random.randint(key_unit, (BLK_DEV,), 0, share)
    return (owner * share + inner).astype(jnp.int32)


def draw_block_unit(key, part):
    key = jax.random.fold_in(key, 11)
    keys = jax.random.split(key, N_SKY * N_TM * N_FOV)
    return jax.vmap(unit_row)(keys).reshape(-1)


def plant(values, stream_key, low, high):
    longest = values.shape.index(max(values.shape))
    spots = []
    for shift in (0, 1):
        where = [jax.random.randint(jax.random.fold_in(stream_key, axis), (), 0, length) for axis, length in enumerate(values.shape)]
        where[longest] = (where[longest] + shift) % values.shape[longest]
        spots.append(tuple(where))
    return values.at[spots[0]].set(low).at[spots[1]].set(high)


def level_of(own_key, shape, shards, smallest, high):
    level = 1.0
    for axis_at, shards_of in shards:
        heights = jax.random.uniform(jax.random.fold_in(jax.random.fold_in(own_key, 6), axis_at), (shards_of,), jnp.float32, smallest / len(shards), high / len(shards))
        level = level * jnp.repeat(jnp.exp(heights), shape[axis_at] // shards_of).reshape((-1,) + (1,) * (len(shape) - 1 - axis_at))
    return level


def gaussian(stream_key, shape, spread, reach, cuts=(), kind=jnp.bfloat16):
    array = jax.random.normal(stream_key, shape, jnp.float32) * spread
    if len(cuts) > 0:
        array = level_of(stream_key, shape, cuts, -0.22, 0.18) * array
    return jnp.clip(array, min=-reach, max=reach).astype(kind)


def setup_inputs(seed: int = 0) -> dict:
    streams_of = jax.random.split(jax.random.key(seed), 10)
    return {
        "src_partials": gaussian(streams_of[0], (BLOCKS, 5, OBS), 0.0625, 0.375, ((0, 32),), jnp.float32),
        "att_partials": gaussian(streams_of[1], (BLOCKS, 4, OBS), 0.05, 0.3, ((0, 32),), jnp.float32),
        "cal_partials": gaussian(streams_of[2], (BLOCKS, OBS), 0.1, 0.6, ((0, 32),), jnp.float32),
        "obs_phase": jnp.clip(1.0 * jax.random.uniform(streams_of[3], (BLOCKS, OBS), jnp.float32) ** level_of(streams_of[3], (BLOCKS, OBS), ((0, 32),), -0.2, 0.2), 0.0, 1.0),
        "obs_residual": gaussian(streams_of[4], (BLOCKS, OBS), 1.0, 6.0, ((0, 32),), jnp.float32),
        "block_source": plant(jax.random.randint(streams_of[5], (BLOCKS,), 0, SRC_DEV), jax.random.fold_in(streams_of[5], 1), 0, SRC_DEV - 1).astype(jnp.int32),
        "block_segment": draw_block_segment(jax.random.fold_in(streams_of[9], 71), 0),
        "block_unit": draw_block_unit(jax.random.fold_in(streams_of[9], 71), 0),
        "live_blocks": draw_live_blocks(jax.random.fold_in(streams_of[9], 71), 0),
    }


index_pairs = [(i, j) for i in range(5) for j in range(i, 5)]

def spline_basis(phase):
    rest = 1.0 - phase
    square = phase * phase
    cubed = square * phase
    return jnp.stack([rest * rest * rest / 6.0, (3.0 * cubed - 6.0 * square + 4.0) / 6.0, (-3.0 * cubed + 3.0 * square + 3.0 * phase + 1.0) / 6.0, cubed / 6.0], axis=1)

def spline_products(residual, partials, phase):
    basis = spline_basis(phase)
    weighted = partials * residual[:, None, :]
    right_side = jnp.einsum('bjo,bco->bjc', basis, weighted, precision=lax.Precision.HIGHEST)
    diag_part = jnp.einsum('bjo,bco->bjc', basis * basis, partials * partials, precision=lax.Precision.HIGHEST)
    return jnp.concatenate([right_side, diag_part], axis=2)

def block_products(partials, residual, live_mask):
    products = jnp.stack([lax.optimization_barrier(jnp.sum(partials[:, i, :] * partials[:, j, :], axis=1)) for i, j in index_pairs], axis=1)
    right_side = lax.optimization_barrier(jnp.sum(partials * residual[:, None, :], axis=2))
    return (products * live_mask[:, None], right_side * live_mask[:, None])

def solve_normals(packed, right_side):
    matrix = {}
    for position, (i, j) in enumerate(index_pairs):
        matrix[i, j] = packed[position] + (1.0 if i == j else 0.0)
    factor = {}
    for i in range(5):
        for j in range(i + 1):
            running = matrix[j, i]
            for k in range(j):
                running = running - factor[i, k] * factor[j, k]
            if i == j:
                factor[i, i] = jnp.sqrt(running)
            else:
                factor[i, j] = running / factor[j, j]
    forward = []
    for i in range(5):
        running = right_side[i]
        for k in range(i):
            running = running - factor[i, k] * forward[k]
        forward.append(running / factor[i, i])
    result = [forward[0]] * 5
    for i in reversed(range(5)):
        running = forward[i]
        for k in range(i + 1, 5):
            running = running - factor[k, i] * result[k]
        result[i] = running / factor[i, i]
    return jnp.stack(result)

def reference(src_partials, att_partials, cal_partials, obs_phase, obs_residual, block_source, block_segment, block_unit, live_blocks):
    block_count = src_partials.shape[0]
    position = jnp.arange(block_count, dtype=jnp.int32)
    device_of = (position // BLK_DEV).astype(jnp.int32)
    live_mask = (position % BLK_DEV < live_blocks[device_of]).astype(jnp.float32)
    sky_of = device_of // (N_TM * N_FOV)
    arc_of = device_of // N_FOV % N_TM
    source_global = (sky_of * SRC_DEV + block_source).astype(jnp.int32)
    products, right_side = block_products(src_partials, obs_residual, live_mask)
    normals = jax.ops.segment_sum(products, source_global, num_segments=SRC).T
    source_right = jax.ops.segment_sum(right_side, source_global, num_segments=SRC).T
    src_update = solve_normals(normals, source_right)
    chosen = src_update[:, source_global].T
    residual = obs_residual - lax.optimization_barrier(jnp.sum(src_partials * chosen[:, :, None], axis=1))
    values = spline_products(residual, att_partials, obs_phase) * live_mask[:, None, None]
    offsets = block_segment[:, None] + jnp.arange(4, dtype=jnp.int32)[None, :]
    knot_total = N_TM * SEG_ARC
    knot_index = jnp.where(offsets < SEG_ARC, arc_of[:, None] * SEG_ARC + offsets, knot_total).astype(jnp.int32)
    knots = jax.ops.segment_sum(values.reshape(-1, 8), knot_index.reshape(-1), num_segments=knot_total + 1)[:knot_total]
    attitude = knots[:, :4] / (1.0 + knots[:, 4:])
    att_update = attitude.T.reshape(4, N_TM, SEG_ARC)
    unit_right = jax.ops.segment_sum(lax.optimization_barrier(jnp.sum(cal_partials * residual, axis=1)) * live_mask, block_unit, num_segments=CAL)
    unit_diag = jax.ops.segment_sum(lax.optimization_barrier(jnp.sum(cal_partials * cal_partials, axis=1)) * live_mask, block_unit, num_segments=CAL)
    cal_update = unit_right / (1.0 + unit_diag)
    return (src_update, att_update, cal_update)
```

```python
import functools

import jax
import jax.numpy as jnp
from jax import lax
from jax.experimental import pallas as pl
from jax.experimental.pallas import tpu as pltpu
from jax.sharding import PartitionSpec as P

SRC_DEV = 4096
SEG_DEV = 128
CAL = 524288
LANES = 128
LOW = 256
F32 = jnp.float32
BF16 = jnp.bfloat16
MESH = pl.DeviceIdType.MESH

index_pairs = [(i, j) for i in range(5) for j in range(i, 5)]
NT = (((1,), (1,)), ((), ()))
NN = (((1,), (0,)), ((), ()))


def split(values):
    first = values.astype(BF16).astype(F32)
    return first, values - first


def one_hot(rows, index):
    grid = lax.broadcasted_iota(jnp.int32, (rows, index.shape[1]), 0)
    return jnp.where(grid == index, 1.0, 0.0).astype(BF16)


def solve_rows(entries):
    matrix = {}
    for position, (i, j) in enumerate(index_pairs):
        matrix[i, j] = entries[position] + (1.0 if i == j else 0.0)
    right_side = entries[15:20]
    factor = {}
    inverse = []
    for j in range(5):
        running = matrix[j, j]
        for k in range(j):
            running = running - factor[j, k] * factor[j, k]
        inverse.append(1.0 / jnp.sqrt(running))
        for i in range(j + 1, 5):
            running = matrix[j, i]
            for k in range(j):
                running = running - factor[i, k] * factor[j, k]
            factor[i, j] = running * inverse[j]
    forward = []
    for i in range(5):
        running = right_side[i]
        for k in range(i):
            running = running - factor[i, k] * forward[k]
        forward.append(running * inverse[i])
    result = [None] * 5
    for i in reversed(range(5)):
        running = forward[i]
        for k in range(i + 1, 5):
            running = running - factor[k, i] * result[k]
        result[i] = running * inverse[i]
    return result


def fold(total):
    return jnp.sum(total, axis=0, keepdims=True)


def kernel(
    sizes,
    src_hbm,
    att_hbm,
    cal_hbm,
    phase_hbm,
    res_hbm,
    source_ref,
    segment_ref,
    unit_ref,
    live_ref,
    src_out,
    att_out,
    cal_out,
    src_in,
    att_in,
    cal_in,
    phase_in,
    res_in,
    src_t,
    att_t,
    basis_t,
    cal_t,
    sums,
    knot_sums,
    unit_sums,
    low_hot,
    spread,
    table,
    table_in,
    update,
    chosen,
    rank_row,
    slot_hot,
    knot_send,
    knot_in,
    unit_send,
    unit_in,
    chunk_sems,
    whole_sems,
    table_sems,
    update_sems,
    knot_sems,
    unit_sems,
):
    n_sky, n_tm, n_fov = sizes
    devices = n_sky * n_tm * n_fov
    blocks = res_hbm.shape[0]
    groups = blocks // LANES
    parts = n_tm * n_fov
    high = SRC_DEV // LOW
    per_part = high // parts
    plane = n_sky * n_fov
    share = CAL // devices
    unit_high = share // LANES

    sky = lax.axis_index("sky")
    tm = lax.axis_index("tm")
    fov = lax.axis_index("fov")
    me = (sky * n_tm + tm) * n_fov + fov
    part_me = tm * n_fov + fov
    plane_me = sky * n_fov + fov

    def any_peer(k):
        q = lax.rem(me + k, devices)
        return (
            lax.div(q, n_tm * n_fov),
            lax.rem(lax.div(q, n_fov), n_tm),
            lax.rem(q, n_fov),
        )

    barrier = pltpu.get_barrier_semaphore()
    for k in range(1, devices):
        pl.semaphore_signal(barrier, inc=1, device_id=any_peer(k), device_id_type=MESH)

    def chunk_copies(g):
        rows = pl.ds(pl.multiple_of(g * LANES, LANES), LANES)
        return (
            pltpu.make_async_copy(src_hbm.at[:, rows], src_in.at[:, rows], chunk_sems.at[0, g]),
            pltpu.make_async_copy(res_hbm.at[rows], res_in.at[rows], chunk_sems.at[1, g]),
        )

    whole_copies = [
        pltpu.make_async_copy(att_hbm, att_in, whole_sems.at[0]),
        pltpu.make_async_copy(cal_hbm, cal_in, whole_sems.at[1]),
        pltpu.make_async_copy(phase_hbm, phase_in, whole_sems.at[2]),
    ]

    def start_chunk(g, carry):
        for copy in chunk_copies(g):
            copy.start()
        return carry

    lax.fori_loop(0, groups, start_chunk, 0)
    for copy in whole_copies:
        copy.start()

    def source_sums(g, carry):
        for copy in chunk_copies(g):
            copy.wait()
        rows = pl.ds(pl.multiple_of(g * LANES, LANES), LANES)
        for c in range(5):
            src_t[g, c] = src_in[c, rows, :].T
        src_t[g, 5] = res_in[rows, :].T
        totals = None
        for t in range(LANES // 8):
            tile = pl.ds(t * 8, 8)
            a = [src_t[g, c, tile, :] for c in range(6)]
            terms = [a[i] * a[j] for i, j in index_pairs] + [a[i] * a[5] for i in range(5)]
            totals = terms if totals is None else [x + y for x, y in zip(totals, terms)]
        for q in range(20):
            sums[q : q + 1, rows] = fold(totals[q])
        return carry

    lax.fori_loop(0, groups, source_sums, 0)
    sums[20:24, :] = jnp.zeros((4, blocks), F32)

    live = lax.broadcasted_iota(jnp.int32, (1, blocks), 1) < live_ref[0]
    source = source_ref[...]
    source_high = source >> 8
    low_hot[...] = one_hot(LOW, source & (LOW - 1))
    pair = jnp.concatenate(split(jnp.where(live, sums[...], 0.0)), axis=0)
    for h in range(high):
        spread[48 * h : 48 * h + 48, :] = jnp.where(source_high == h, pair, 0.0).astype(BF16)
    placed = lax.dot_general(
        spread[: 48 * high, :], low_hot[...], NT, preferred_element_type=F32
    )
    for h in range(high):
        table[h // per_part, h % per_part] = (
            placed[48 * h : 48 * h + 24] + placed[48 * h + 24 : 48 * h + 48]
        )

    pl.semaphore_wait(barrier, devices - 1)

    table_copies = []
    for k in range(1, parts):
        p = lax.rem(part_me + k, parts)
        copy = pltpu.make_async_remote_copy(
            src_ref=table.at[p],
            dst_ref=table_in.at[k],
            send_sem=table_sems.at[0, k],
            recv_sem=table_sems.at[1, k],
            device_id=(sky, lax.div(p, n_fov), lax.rem(p, n_fov)),
            device_id_type=MESH,
        )
        copy.start()
        table_copies.append(copy)

    for copy in whole_copies:
        copy.wait()

    def fixed_sums(g, carry):
        rows = pl.ds(pl.multiple_of(g * LANES, LANES), LANES)
        for c in range(4):
            att_t[g, c] = att_in[rows, c, :].T
        cal_t[g] = cal_in[rows, :].T
        phase_t = phase_in[rows, :].T
        rest = 1.0 - phase_t
        square = phase_t * phase_t
        cubed = square * phase_t
        basis_t[g, 0] = rest * rest * rest * (1.0 / 6.0)
        basis_t[g, 1] = (3.0 * cubed - 6.0 * square + 4.0) * (1.0 / 6.0)
        basis_t[g, 2] = (-3.0 * cubed + 3.0 * square + 3.0 * phase_t + 1.0) * (1.0 / 6.0)
        basis_t[g, 3] = cubed * (1.0 / 6.0)
        totals = None
        for t in range(LANES // 8):
            tile = pl.ds(t * 8, 8)
            b = [basis_t[g, j, tile, :] for j in range(4)]
            h = [att_t[g, c, tile, :] for c in range(4)]
            b = [x * x for x in b]
            h = [x * x for x in h]
            u = cal_t[g, tile, :]
            terms = [b[j] * h[c] for j in range(4) for c in range(4)] + [u * u]
            totals = terms if totals is None else [x + y for x, y in zip(totals, terms)]
        for j in range(4):
            for c in range(4):
                q = j * 8 + 4 + c
                knot_sums[q : q + 1, rows] = fold(totals[j * 4 + c])
        unit_sums[1:2, rows] = fold(totals[16])
        return carry

    lax.fori_loop(0, groups, fixed_sums, 0)

    unit = unit_ref[...]
    owner = lax.div(unit, share)
    local = unit - owner * share
    row = lax.broadcasted_iota(jnp.int32, (LANES, 2 * LANES), 0)
    column = lax.broadcasted_iota(jnp.int32, (LANES, 2 * LANES), 1)
    ramp = jnp.where(row <= column, 1.0, 0.0).astype(BF16)
    before = jnp.zeros((devices, LANES), F32)
    for g in range(groups):
        cut = slice(g * LANES, (g + 1) * LANES)
        hot = lax.broadcasted_iota(jnp.int32, (devices, LANES), 0) == owner[:, cut]
        hot = jnp.where(hot, 1.0, 0.0)
        counts = lax.dot_general(hot.astype(BF16), ramp, NN, preferred_element_type=F32)
        rank_row[:, cut] = fold(hot * (counts[:, :LANES] + before)) - 1.0
        before = before + counts[:, LANES:]
    slot_hot[...] = one_hot(LANES, rank_row[...].astype(jnp.int32))

    for copy in table_copies:
        copy.wait_recv()
    for s in range(per_part):
        total = table[part_me, s]
        for k in range(1, parts):
            total = total + table_in[k, s]
        solved = solve_rows([total[q : q + 1] for q in range(20)])
        for c in range(5):
            update[part_me, s, c : c + 1, :] = solved[c]
        update[part_me, s, 5:8, :] = jnp.zeros((3, LOW), F32)

    update_copies = []
    for k in range(1, parts):
        p = lax.rem(part_me + k, parts)
        copy = pltpu.make_async_remote_copy(
            src_ref=update.at[part_me],
            dst_ref=update.at[part_me],
            send_sem=update_sems.at[0, k],
            recv_sem=update_sems.at[1, k],
            device_id=(sky, lax.div(p, n_fov), lax.rem(p, n_fov)),
            device_id_type=MESH,
        )
        copy.start()
        update_copies.append(copy)
    for k in range(1, parts):
        p = lax.rem(part_me + parts - k, parts)
        pltpu.make_async_remote_copy(
            src_ref=update.at[part_me],
            dst_ref=update.at[p],
            send_sem=update_sems.at[0, k],
            recv_sem=update_sems.at[1, k],
            device_id=(sky, lax.div(p, n_fov), lax.rem(p, n_fov)),
            device_id_type=MESH,
        ).wait_recv()

    pieces = []
    for h in range(high):
        piece = update[h // per_part, h % per_part]
        src_out[:, h * LOW : (h + 1) * LOW] = piece[:5]
        pieces.extend(split(piece))
    picked = lax.dot_general(
        jnp.concatenate(pieces, axis=0).astype(BF16),
        low_hot[...],
        NN,
        preferred_element_type=F32,
    )
    total = jnp.zeros((8, blocks), F32)
    for h in range(high):
        piece = picked[16 * h : 16 * h + 8] + picked[16 * h + 8 : 16 * h + 16]
        total = jnp.where(source_high == h, piece, total)
    chosen[...] = total

    def residual_sums(g, carry):
        rows = pl.ds(pl.multiple_of(g * LANES, LANES), LANES)
        x = [jnp.broadcast_to(chosen[c : c + 1, rows], (8, LANES)) for c in range(5)]
        totals = None
        for t in range(LANES // 8):
            tile = pl.ds(t * 8, 8)
            taken = src_t[g, 0, tile, :] * x[0]
            for c in range(1, 5):
                taken = taken + src_t[g, c, tile, :] * x[c]
            residual = src_t[g, 5, tile, :] - taken
            b = [basis_t[g, j, tile, :] for j in range(4)]
            h = [att_t[g, c, tile, :] * residual for c in range(4)]
            terms = [b[j] * h[c] for j in range(4) for c in range(4)]
            terms.append(cal_t[g, tile, :] * residual)
            totals = terms if totals is None else [x_ + y_ for x_, y_ in zip(totals, terms)]
        for j in range(4):
            for c in range(4):
                q = j * 8 + c
                knot_sums[q : q + 1, rows] = fold(totals[j * 4 + c])
        unit_sums[0:1, rows] = fold(totals[16])
        return carry

    lax.fori_loop(0, groups, residual_sums, 0)

    unit_pair = jnp.where(live, unit_sums[0:2, :], 0.0)
    first, second = split(unit_pair)
    local_high = (local >> 7).astype(F32)
    local_low = (local & (LANES - 1)).astype(F32)
    fields = jnp.concatenate(
        [first, local_high, local_low, second, jnp.zeros((2, blocks), F32)], axis=0
    )
    for o in range(0, devices, 2):
        both = [jnp.where(owner == o + i, fields, 0.0) for i in range(2)]
        spread[8 * o : 8 * o + 16, :] = jnp.concatenate(both, axis=0).astype(BF16)
    packed = lax.dot_general(
        spread[: 8 * devices, :], slot_hot[...], NT, preferred_element_type=F32
    )
    for o in range(devices):
        unit_send[o] = packed[8 * o : 8 * o + 4] + packed[8 * o + 4 : 8 * o + 8]

    unit_copies = []
    for k in range(1, devices):
        copy = pltpu.make_async_remote_copy(
            src_ref=unit_send.at[lax.rem(me + k, devices)],
            dst_ref=unit_in.at[k],
            send_sem=unit_sems.at[0, k],
            recv_sem=unit_sems.at[1, k],
            device_id=any_peer(k),
            device_id_type=MESH,
        )
        copy.start()
        unit_copies.append(copy)

    segment = segment_ref[...]
    segment_high = segment >> 7
    segment_hot = one_hot(SEG_DEV, segment & (SEG_DEV - 1))
    pair = jnp.concatenate(split(jnp.where(live, knot_sums[...], 0.0)), axis=0)
    for h in range(n_sky):
        spread[64 * h : 64 * h + 64, :] = jnp.where(segment_high == h, pair, 0.0).astype(BF16)
    placed = lax.dot_general(
        spread[: 64 * n_sky, :], segment_hot, NT, preferred_element_type=F32
    )
    wide = jnp.concatenate(
        [placed[64 * h : 64 * h + 32] + placed[64 * h + 32 : 64 * h + 64] for h in range(n_sky)],
        axis=1,
    )
    knots = wide[0:8]
    position = lax.broadcasted_iota(jnp.int32, knots.shape, 1)
    for j in range(1, 4):
        moved = pltpu.roll(wide[8 * j : 8 * j + 8], j, 1)
        knots = knots + jnp.where(position >= j, moved, 0.0)
    for h in range(n_sky):
        knot_send[h] = knots[:, h * SEG_DEV : (h + 1) * SEG_DEV]

    knot_copies = []
    for k in range(1, plane):
        q = lax.rem(plane_me + k, plane)
        peer_sky = lax.div(q, n_fov)
        copy = pltpu.make_async_remote_copy(
            src_ref=knot_send.at[peer_sky],
            dst_ref=knot_in.at[k],
            send_sem=knot_sems.at[0, k],
            recv_sem=knot_sems.at[1, k],
            device_id=(peer_sky, tm, lax.rem(q, n_fov)),
            device_id_type=MESH,
        )
        copy.start()
        knot_copies.append(copy)

    for copy in unit_copies:
        copy.wait_recv()
    unit_in[0] = unit_send[me]
    flat = jnp.concatenate([unit_in[k] for k in range(devices)], axis=1)
    first, second = split(flat[0:2])
    flat_high = flat[2:3].astype(jnp.int32)
    flat_low = flat[3:4].astype(jnp.int32)
    high_hit = (
        lax.broadcasted_iota(jnp.int32, (unit_high, flat.shape[1]), 0) == flat_high
    )
    rows = [first[0:1], second[0:1], first[1:2], second[1:2]]
    spread_units = jnp.concatenate(
        [jnp.where(high_hit, value, 0.0).astype(BF16) for value in rows], axis=0
    )
    units = lax.dot_general(
        spread_units, one_hot(LANES, flat_low), NT, preferred_element_type=F32
    )
    n = unit_high
    cal_out[...] = (units[:n] + units[n : 2 * n]) / (
        1.0 + (units[2 * n : 3 * n] + units[3 * n :])
    )

    for copy in knot_copies:
        copy.wait_recv()
    total = knot_send[sky]
    for k in range(1, plane):
        total = total + knot_in[k]
    att_out[...] = total[0:4] / (1.0 + total[4:8])

    for copy in table_copies + update_copies + unit_copies + knot_copies:
        copy.wait_send()


def shards(sizes, src, att, cal, phase, res, source, segment, unit, live):
    n_sky, n_tm, n_fov = sizes
    devices = n_sky * n_tm * n_fov
    blocks = src.shape[0]
    groups = blocks // LANES
    parts = n_tm * n_fov
    plane = n_sky * n_fov
    high = SRC_DEV // LOW
    per_part = high // parts
    spread_rows = max(48 * high, 8 * devices, 64 * n_sky)
    anywhere = pl.BlockSpec(memory_space=pl.ANY)
    vmem = pl.BlockSpec(memory_space=pltpu.VMEM)
    smem = pl.BlockSpec(memory_space=pltpu.SMEM)
    dma = pltpu.SemaphoreType.DMA
    src_update, att_update, cal_update = pl.pallas_call(
        functools.partial(kernel, sizes),
        out_shape=(
            jax.ShapeDtypeStruct((5, SRC_DEV), F32),
            jax.ShapeDtypeStruct((4, SEG_DEV), F32),
            jax.ShapeDtypeStruct((CAL // devices // LANES, LANES), F32),
        ),
        in_specs=[anywhere] * 5 + [vmem] * 3 + [smem],
        out_specs=(vmem, vmem, vmem),
        scratch_shapes=[
            pltpu.VMEM((src.shape[1], blocks, LANES), F32),
            pltpu.VMEM(att.shape, F32),
            pltpu.VMEM(cal.shape, F32),
            pltpu.VMEM(phase.shape, F32),
            pltpu.VMEM(res.shape, F32),
            pltpu.VMEM((groups, 6, LANES, LANES), F32),
            pltpu.VMEM((groups, 4, LANES, LANES), F32),
            pltpu.VMEM((groups, 4, LANES, LANES), F32),
            pltpu.VMEM((groups, LANES, LANES), F32),
            pltpu.VMEM((24, blocks), F32),
            pltpu.VMEM((32, blocks), F32),
            pltpu.VMEM((8, blocks), F32),
            pltpu.VMEM((LOW, blocks), BF16),
            pltpu.VMEM((spread_rows, blocks), BF16),
            pltpu.VMEM((parts, per_part, 24, LOW), F32),
            pltpu.VMEM((parts, per_part, 24, LOW), F32),
            pltpu.VMEM((parts, per_part, 8, LOW), F32),
            pltpu.VMEM((8, blocks), F32),
            pltpu.VMEM((1, blocks), F32),
            pltpu.VMEM((LANES, blocks), BF16),
            pltpu.VMEM((n_sky, 8, SEG_DEV), F32),
            pltpu.VMEM((plane, 8, SEG_DEV), F32),
            pltpu.VMEM((devices, 4, LANES), F32),
            pltpu.VMEM((devices, 4, LANES), F32),
            dma((2, groups)),
            dma((3,)),
            dma((2, parts)),
            dma((2, parts)),
            dma((2, plane)),
            dma((2, devices)),
        ],
        compiler_params=pltpu.CompilerParams(
            collective_id=0, has_side_effects=True, vmem_limit_bytes=58 * 1024 * 1024
        ),
    )(
        jnp.transpose(src, (1, 0, 2)),
        att,
        cal,
        phase,
        res,
        source.reshape(1, blocks),
        segment.reshape(1, blocks),
        unit.reshape(1, blocks),
        live,
    )
    return (
        src_update,
        att_update.reshape(4, 1, SEG_DEV),
        cal_update.reshape(CAL // devices),
    )


def solution(mesh):
    sizes = (mesh.shape["sky"], mesh.shape["tm"], mesh.shape["fov"])
    every = ("sky", "tm", "fov")
    return jax.shard_map(
        functools.partial(shards, sizes),
        mesh=mesh,
        in_specs=(
            P(every, None, None),
            P(every, None, None),
            P(every, None),
            P(every, None),
            P(every, None),
            P(every),
            P(every),
            P(every),
            P(every),
        ),
        out_specs=(P(None, "sky"), P(None, "tm", "sky"), P(every)),
        check_vma=False,
    )
```

```python
import functools

import jax
import jax.numpy as jnp
from jax import lax
from jax.experimental import pallas as pl
from jax.experimental.pallas import tpu as pltpu
from jax.sharding import PartitionSpec as P

SRC_DEV = 4096
SEG_DEV = 128
CAL = 524288
LANES = 128
LOW = 256
F32 = jnp.float32
BF16 = jnp.bfloat16
MESH = pl.DeviceIdType.MESH

index_pairs = [(i, j) for i in range(5) for j in range(i, 5)]
NT = (((1,), (1,)), ((), ()))
NN = (((1,), (0,)), ((), ()))


def split(values):
    first = values.astype(BF16).astype(F32)
    return first, values - first


def one_hot(rows, index):
    grid = lax.broadcasted_iota(jnp.int32, (rows, index.shape[1]), 0)
    return jnp.where(grid == index, 1.0, 0.0).astype(BF16)


def solve_rows(entries):
    matrix = {}
    for position, (i, j) in enumerate(index_pairs):
        matrix[i, j] = entries[position] + (1.0 if i == j else 0.0)
    right_side = entries[15:20]
    factor = {}
    inverse = []
    for j in range(5):
        running = matrix[j, j]
        for k in range(j):
            running = running - factor[j, k] * factor[j, k]
        inverse.append(1.0 / jnp.sqrt(running))
        for i in range(j + 1, 5):
            running = matrix[j, i]
            for k in range(j):
                running = running - factor[i, k] * factor[j, k]
            factor[i, j] = running * inverse[j]
    forward = []
    for i in range(5):
        running = right_side[i]
        for k in range(i):
            running = running - factor[i, k] * forward[k]
        forward.append(running * inverse[i])
    result = [None] * 5
    for i in reversed(range(5)):
        running = forward[i]
        for k in range(i + 1, 5):
            running = running - factor[k, i] * result[k]
        result[i] = running * inverse[i]
    return result


def fold(total):
    return jnp.sum(total, axis=0, keepdims=True)


def kernel(
    sizes,
    src_hbm,
    att_hbm,
    cal_hbm,
    phase_hbm,
    res_hbm,
    source_ref,
    segment_ref,
    unit_ref,
    live_ref,
    src_out,
    knot_out,
    unit_out,
    src_in,
    att_in,
    cal_in,
    phase_in,
    res_in,
    src_t,
    att_t,
    basis_t,
    cal_t,
    sums,
    knot_sums,
    unit_sums,
    low_hot,
    spread,
    table,
    fov_in,
    half,
    table_in,
    total_ref,
    update,
    chosen,
    rank_row,
    slot_hot,
    knot_send,
    knot_in,
    unit_send,
    unit_in,
    chunk_sems,
    whole_sems,
    fov_sems,
    table_sems,
    update_sems,
    knot_sems,
    unit_sems,
):
    n_sky, n_tm, n_fov = sizes
    devices = n_sky * n_tm * n_fov
    blocks = res_hbm.shape[0]
    groups = blocks // LANES
    parts = n_tm * n_fov
    high = SRC_DEV // LOW
    per_part = high // parts
    plane = n_sky * n_fov
    share = CAL // devices
    cuts = SRC_DEV // parts // LANES

    sky = lax.axis_index("sky")
    tm = lax.axis_index("tm")
    fov = lax.axis_index("fov")
    me = (sky * n_tm + tm) * n_fov + fov
    part_me = fov * n_tm + tm
    plane_me = sky * n_fov + fov

    def any_peer(k):
        q = lax.rem(me + k, devices)
        return (
            lax.div(q, n_tm * n_fov),
            lax.rem(lax.div(q, n_fov), n_tm),
            lax.rem(q, n_fov),
        )

    def chunk_copies(g):
        rows = pl.ds(pl.multiple_of(g * LANES, LANES), LANES)
        return (
            pltpu.make_async_copy(src_hbm.at[:, rows], src_in.at[:, rows], chunk_sems.at[0, g]),
            pltpu.make_async_copy(res_hbm.at[rows], res_in.at[rows], chunk_sems.at[1, g]),
        )

    whole_copies = [
        pltpu.make_async_copy(att_hbm, att_in, whole_sems.at[0]),
        pltpu.make_async_copy(cal_hbm, cal_in, whole_sems.at[1]),
        pltpu.make_async_copy(phase_hbm, phase_in, whole_sems.at[2]),
    ]

    def start_chunk(g, carry):
        for copy in chunk_copies(g):
            copy.start()
        return carry

    lax.fori_loop(0, groups, start_chunk, 0)
    for copy in whole_copies:
        copy.start()

    barrier = pltpu.get_barrier_semaphore()
    for k in range(1, devices):
        pl.semaphore_signal(barrier, inc=1, device_id=any_peer(k), device_id_type=MESH)

    source = source_ref[...]
    source_high = source >> 8
    low_hot[...] = one_hot(LOW, source & (LOW - 1))

    def source_sums(g, carry):
        for copy in chunk_copies(g):
            copy.wait()
        rows = pl.ds(pl.multiple_of(g * LANES, LANES), LANES)
        for c in range(5):
            src_t[g, c] = src_in[c, rows, :].T
        src_t[g, 5] = res_in[rows, :].T
        totals = None
        for t in range(LANES // 8):
            tile = pl.ds(t * 8, 8)
            a = [src_t[g, c, tile, :] for c in range(6)]
            terms = [a[i] * a[j] for i, j in index_pairs] + [a[i] * a[5] for i in range(5)]
            totals = terms if totals is None else [x + y for x, y in zip(totals, terms)]
        for q in range(20):
            sums[q : q + 1, rows] = fold(totals[q])
        return carry

    lax.fori_loop(0, groups, source_sums, 0)
    sums[20:24, :] = jnp.zeros((4, blocks), F32)

    live = lax.broadcasted_iota(jnp.int32, (1, blocks), 1) < live_ref[0]
    pair = jnp.concatenate(split(jnp.where(live, sums[...], 0.0)), axis=0)
    for h in range(high):
        spread[48 * h : 48 * h + 48, :] = jnp.where(source_high == h, pair, 0.0).astype(BF16)
    placed = lax.dot_general(
        spread[: 48 * high, :], low_hot[...], NT, preferred_element_type=F32
    )
    for h in range(high):
        piece = placed[48 * h : 48 * h + 24] + placed[48 * h + 24 : 48 * h + 48]
        p = h // per_part
        for l in range(LOW // LANES):
            row = ((h % per_part) * (LOW // LANES) + l) * 20
            table[p // n_tm, p % n_tm, row : row + 20, :] = piece[
                :20, l * LANES : (l + 1) * LANES
            ]

    pl.semaphore_wait(barrier, devices - 1)

    fov_copies = []
    for k in range(1, n_fov):
        f = lax.rem(fov + k, n_fov)
        copy = pltpu.make_async_remote_copy(
            src_ref=table.at[f],
            dst_ref=fov_in.at[k],
            send_sem=fov_sems.at[0, k],
            recv_sem=fov_sems.at[1, k],
            device_id=(sky, tm, f),
            device_id_type=MESH,
        )
        copy.start()
        fov_copies.append(copy)

    for copy in whole_copies:
        copy.wait()

    def fixed_sums(g, carry):
        rows = pl.ds(pl.multiple_of(g * LANES, LANES), LANES)
        for c in range(4):
            att_t[g, c] = att_in[rows, c, :].T
        cal_t[g] = cal_in[rows, :].T
        phase_t = phase_in[rows, :].T
        rest = 1.0 - phase_t
        square = phase_t * phase_t
        cubed = square * phase_t
        basis_t[g, 0] = rest * rest * rest * (1.0 / 6.0)
        basis_t[g, 1] = (3.0 * cubed - 6.0 * square + 4.0) * (1.0 / 6.0)
        basis_t[g, 2] = (-3.0 * cubed + 3.0 * square + 3.0 * phase_t + 1.0) * (1.0 / 6.0)
        basis_t[g, 3] = cubed * (1.0 / 6.0)
        totals = None
        for t in range(LANES // 8):
            tile = pl.ds(t * 8, 8)
            b = [basis_t[g, j, tile, :] for j in range(4)]
            h = [att_t[g, c, tile, :] for c in range(4)]
            b = [x * x for x in b]
            h = [x * x for x in h]
            u = cal_t[g, tile, :]
            terms = [b[j] * h[c] for j in range(4) for c in range(4)] + [u * u]
            totals = terms if totals is None else [x + y for x, y in zip(totals, terms)]
        for j in range(4):
            for c in range(4):
                q = j * 8 + 4 + c
                knot_sums[q : q + 1, rows] = fold(totals[j * 4 + c])
        unit_sums[1:2, rows] = fold(totals[16])
        return carry

    lax.fori_loop(0, groups // 4, fixed_sums, 0)

    for copy in fov_copies:
        copy.wait_recv()
    for t in range(n_tm):
        total = table[fov, t]
        for k in range(1, n_fov):
            total = total + fov_in[k, t]
        half[t] = total
    table_copies = []
    for k in range(1, n_tm):
        t = lax.rem(tm + k, n_tm)
        copy = pltpu.make_async_remote_copy(
            src_ref=half.at[t],
            dst_ref=table_in.at[k],
            send_sem=table_sems.at[0, k],
            recv_sem=table_sems.at[1, k],
            device_id=(sky, t, fov),
            device_id_type=MESH,
        )
        copy.start()
        table_copies.append(copy)

    lax.fori_loop(groups // 4, groups, fixed_sums, 0)

    for copy in table_copies:
        copy.wait_recv()
    total = half[tm]
    for k in range(1, n_tm):
        total = total + table_in[k]
    total_ref[...] = total
    solved = solve_rows([total_ref[pl.ds(q, cuts, stride=20), :] for q in range(20)])
    for c in range(5):
        update[part_me, c * cuts : (c + 1) * cuts, :] = solved[c]

    update_copies = []
    for k in range(1, parts):
        p = lax.rem(part_me + k, parts)
        copy = pltpu.make_async_remote_copy(
            src_ref=update.at[part_me],
            dst_ref=update.at[part_me],
            send_sem=update_sems.at[0, k],
            recv_sem=update_sems.at[1, k],
            device_id=(sky, lax.rem(p, n_tm), lax.div(p, n_tm)),
            device_id_type=MESH,
        )
        copy.start()
        update_copies.append(copy)

    unit = unit_ref[...]
    owner = lax.div(unit, share)
    local = unit - owner * share
    row = lax.broadcasted_iota(jnp.int32, (LANES, 2 * LANES), 0)
    column = lax.broadcasted_iota(jnp.int32, (LANES, 2 * LANES), 1)
    ramp = jnp.where(row <= column, 1.0, 0.0).astype(BF16)
    before = jnp.zeros((devices, LANES), F32)
    for g in range(groups):
        cut = slice(g * LANES, (g + 1) * LANES)
        hot = lax.broadcasted_iota(jnp.int32, (devices, LANES), 0) == owner[:, cut]
        hot = jnp.where(hot, 1.0, 0.0)
        counts = lax.dot_general(hot.astype(BF16), ramp, NN, preferred_element_type=F32)
        rank_row[:, cut] = fold(hot * (counts[:, :LANES] + before)) - 1.0
        before = before + counts[:, LANES:]
    slot_hot[...] = one_hot(LANES, rank_row[...].astype(jnp.int32))

    for k in range(1, parts):
        p = lax.rem(part_me + parts - k, parts)
        pltpu.make_async_remote_copy(
            src_ref=update.at[part_me],
            dst_ref=update.at[p],
            send_sem=update_sems.at[0, k],
            recv_sem=update_sems.at[1, k],
            device_id=(sky, lax.rem(p, n_tm), lax.div(p, n_tm)),
            device_id_type=MESH,
        ).wait_recv()

    pieces = []
    for h in range(high):
        start = (h % per_part) * (LOW // LANES)
        piece = jnp.concatenate(
            [
                update[h // per_part, pl.ds(start + l, 5, stride=cuts), :]
                for l in range(LOW // LANES)
            ],
            axis=1,
        )
        src_out[:, h * LOW : (h + 1) * LOW] = piece
        pieces.extend(split(jnp.concatenate([piece, jnp.zeros((3, LOW), F32)], axis=0)))
    picked = lax.dot_general(
        jnp.concatenate(pieces, axis=0).astype(BF16),
        low_hot[...],
        NN,
        preferred_element_type=F32,
    )
    total = jnp.zeros((8, blocks), F32)
    for h in range(high):
        piece = picked[16 * h : 16 * h + 8] + picked[16 * h + 8 : 16 * h + 16]
        total = jnp.where(source_high == h, piece, total)
    chosen[...] = total

    def residual_sums(g, carry):
        rows = pl.ds(pl.multiple_of(g * LANES, LANES), LANES)
        x = [jnp.broadcast_to(chosen[c : c + 1, rows], (8, LANES)) for c in range(5)]
        totals = None
        for t in range(LANES // 8):
            tile = pl.ds(t * 8, 8)
            taken = src_t[g, 0, tile, :] * x[0]
            for c in range(1, 5):
                taken = taken + src_t[g, c, tile, :] * x[c]
            residual = src_t[g, 5, tile, :] - taken
            b = [basis_t[g, j, tile, :] for j in range(4)]
            h = [att_t[g, c, tile, :] * residual for c in range(4)]
            terms = [b[j] * h[c] for j in range(4) for c in range(4)]
            terms.append(cal_t[g, tile, :] * residual)
            totals = terms if totals is None else [x_ + y_ for x_, y_ in zip(totals, terms)]
        for j in range(4):
            for c in range(4):
                q = j * 8 + c
                knot_sums[q : q + 1, rows] = fold(totals[j * 4 + c])
        unit_sums[0:1, rows] = fold(totals[16])
        return carry

    lax.fori_loop(0, groups, residual_sums, 0)

    unit_pair = jnp.where(live, unit_sums[0:2, :], 0.0)
    first, second = split(unit_pair)
    local_high = (local >> 7).astype(F32)
    local_low = (local & (LANES - 1)).astype(F32)
    fields = jnp.concatenate(
        [first, local_high, local_low, second, jnp.zeros((2, blocks), F32)], axis=0
    )
    for o in range(0, devices, 2):
        both = [jnp.where(owner == o + i, fields, 0.0) for i in range(2)]
        spread[8 * o : 8 * o + 16, :] = jnp.concatenate(both, axis=0).astype(BF16)
    packed = lax.dot_general(
        spread[: 8 * devices, :], slot_hot[...], NT, preferred_element_type=F32
    )
    for o in range(devices):
        unit_send[o] = packed[8 * o : 8 * o + 4] + packed[8 * o + 4 : 8 * o + 8]

    unit_copies = []
    for k in range(1, devices):
        copy = pltpu.make_async_remote_copy(
            src_ref=unit_send.at[lax.rem(me + k, devices)],
            dst_ref=unit_in.at[k],
            send_sem=unit_sems.at[0, k],
            recv_sem=unit_sems.at[1, k],
            device_id=any_peer(k),
            device_id_type=MESH,
        )
        copy.start()
        unit_copies.append(copy)

    segment = segment_ref[...]
    segment_high = segment >> 7
    segment_hot = one_hot(SEG_DEV, segment & (SEG_DEV - 1))
    pair = jnp.concatenate(split(jnp.where(live, knot_sums[...], 0.0)), axis=0)
    for h in range(n_sky):
        spread[64 * h : 64 * h + 64, :] = jnp.where(segment_high == h, pair, 0.0).astype(BF16)
    placed = lax.dot_general(
        spread[: 64 * n_sky, :], segment_hot, NT, preferred_element_type=F32
    )
    wide = jnp.concatenate(
        [placed[64 * h : 64 * h + 32] + placed[64 * h + 32 : 64 * h + 64] for h in range(n_sky)],
        axis=1,
    )
    knots = wide[0:8]
    position = lax.broadcasted_iota(jnp.int32, knots.shape, 1)
    for j in range(1, 4):
        moved = pltpu.roll(wide[8 * j : 8 * j + 8], j, 1)
        knots = knots + jnp.where(position >= j, moved, 0.0)
    for h in range(n_sky):
        knot_send[h] = knots[:, h * SEG_DEV : (h + 1) * SEG_DEV]

    knot_copies = []
    for k in range(1, plane):
        q = lax.rem(plane_me + k, plane)
        peer_sky = lax.div(q, n_fov)
        copy = pltpu.make_async_remote_copy(
            src_ref=knot_send.at[peer_sky],
            dst_ref=knot_in.at[k],
            send_sem=knot_sems.at[0, k],
            recv_sem=knot_sems.at[1, k],
            device_id=(peer_sky, tm, lax.rem(q, n_fov)),
            device_id_type=MESH,
        )
        copy.start()
        knot_copies.append(copy)

    for copy in unit_copies:
        copy.wait_recv()
    unit_in[0] = unit_send[me]
    unit_out[...] = jnp.concatenate([unit_in[k] for k in range(devices)], axis=1)

    for copy in knot_copies:
        copy.wait_recv()
    total = knot_send[sky]
    for k in range(1, plane):
        total = total + knot_in[k]
    knot_out[...] = total

    for copy in fov_copies + table_copies + update_copies + unit_copies + knot_copies:
        copy.wait_send()


def finish(src_ref, knot_ref, unit_ref, src_out, att_out, cal_out):
    src_out[...] = src_ref[...]
    att_out[...] = knot_ref[0:4] / (1.0 + knot_ref[4:8])
    n = cal_out.shape[0]
    first, second = split(unit_ref[0:2])
    flat_high = unit_ref[2:3].astype(jnp.int32)
    flat_low = unit_ref[3:4].astype(jnp.int32)
    high_hit = lax.broadcasted_iota(jnp.int32, (n, unit_ref.shape[1]), 0) == flat_high
    rows = [first[0:1], second[0:1], first[1:2], second[1:2]]
    spread_units = jnp.concatenate(
        [jnp.where(high_hit, value, 0.0).astype(BF16) for value in rows], axis=0
    )
    units = lax.dot_general(
        spread_units, one_hot(LANES, flat_low), NT, preferred_element_type=F32
    )
    cal_out[...] = (units[:n] + units[n : 2 * n]) / (
        1.0 + (units[2 * n : 3 * n] + units[3 * n :])
    )


def shards(sizes, src, att, cal, phase, res, source, segment, unit, live):
    n_sky, n_tm, n_fov = sizes
    devices = n_sky * n_tm * n_fov
    blocks = src.shape[0]
    groups = blocks // LANES
    parts = n_tm * n_fov
    plane = n_sky * n_fov
    high = SRC_DEV // LOW
    cuts = SRC_DEV // parts // LANES
    spread_rows = max(48 * high, 8 * devices, 64 * n_sky)
    anywhere = pl.BlockSpec(memory_space=pl.ANY)
    vmem = pl.BlockSpec(memory_space=pltpu.VMEM)
    smem = pl.BlockSpec(memory_space=pltpu.SMEM)
    dma = pltpu.SemaphoreType.DMA
    updates, knots, units = pl.pallas_call(
        functools.partial(kernel, sizes),
        out_shape=(
            jax.ShapeDtypeStruct((5, SRC_DEV), F32),
            jax.ShapeDtypeStruct((8, SEG_DEV), F32),
            jax.ShapeDtypeStruct((4, devices * LANES), F32),
        ),
        in_specs=[anywhere] * 5 + [vmem] * 3 + [smem],
        out_specs=(vmem, vmem, vmem),
        scratch_shapes=[
            pltpu.VMEM((src.shape[1], blocks, LANES), F32),
            pltpu.VMEM(att.shape, F32),
            pltpu.VMEM(cal.shape, F32),
            pltpu.VMEM(phase.shape, F32),
            pltpu.VMEM(res.shape, F32),
            pltpu.VMEM((groups, 6, LANES, LANES), F32),
            pltpu.VMEM((groups, 4, LANES, LANES), F32),
            pltpu.VMEM((groups, 4, LANES, LANES), F32),
            pltpu.VMEM((groups, LANES, LANES), F32),
            pltpu.VMEM((24, blocks), F32),
            pltpu.VMEM((32, blocks), F32),
            pltpu.VMEM((8, blocks), F32),
            pltpu.VMEM((LOW, blocks), BF16),
            pltpu.VMEM((spread_rows, blocks), BF16),
            pltpu.VMEM((n_fov, n_tm, 20 * cuts, LANES), F32),
            pltpu.VMEM((n_fov, n_tm, 20 * cuts, LANES), F32),
            pltpu.VMEM((n_tm, 20 * cuts, LANES), F32),
            pltpu.VMEM((n_tm, 20 * cuts, LANES), F32),
            pltpu.VMEM((20 * cuts, LANES), F32),
            pltpu.VMEM((parts, 5 * cuts, LANES), F32),
            pltpu.VMEM((8, blocks), F32),
            pltpu.VMEM((1, blocks), F32),
            pltpu.VMEM((LANES, blocks), BF16),
            pltpu.VMEM((n_sky, 8, SEG_DEV), F32),
            pltpu.VMEM((plane, 8, SEG_DEV), F32),
            pltpu.VMEM((devices, 4, LANES), F32),
            pltpu.VMEM((devices, 4, LANES), F32),
            dma((2, groups)),
            dma((3,)),
            dma((2, n_fov)),
            dma((2, n_tm)),
            dma((2, parts)),
            dma((2, plane)),
            dma((2, devices)),
        ],
        compiler_params=pltpu.CompilerParams(
            collective_id=0, has_side_effects=True, vmem_limit_bytes=58 * 1024 * 1024
        ),
    )(
        jnp.transpose(src, (1, 0, 2)),
        att,
        cal,
        phase,
        res,
        source.reshape(1, blocks),
        segment.reshape(1, blocks),
        unit.reshape(1, blocks),
        live,
    )
    src_update, att_update, cal_update = pl.pallas_call(
        finish,
        out_shape=(
            jax.ShapeDtypeStruct((5, SRC_DEV), F32),
            jax.ShapeDtypeStruct((4, SEG_DEV), F32),
            jax.ShapeDtypeStruct((CAL // devices // LANES, LANES), F32),
        ),
        in_specs=[vmem] * 3,
        out_specs=(vmem, vmem, vmem),
        compiler_params=pltpu.CompilerParams(vmem_limit_bytes=40 * 1024 * 1024),
    )(updates, knots, units)
    return (
        src_update,
        att_update.reshape(4, 1, SEG_DEV),
        cal_update.reshape(CAL // devices),
    )


def solution(mesh):
    sizes = (mesh.shape["sky"], mesh.shape["tm"], mesh.shape["fov"])
    every = ("sky", "tm", "fov")
    return jax.shard_map(
        functools.partial(shards, sizes),
        mesh=mesh,
        in_specs=(
            P(every, None, None),
            P(every, None, None),
            P(every, None),
            P(every, None),
            P(every, None),
            P(every),
            P(every),
            P(every),
            P(every),
        ),
        out_specs=(P(None, "sky"), P(None, "tm", "sky"), P(every)),
        check_vma=False,
    )
```

```python
import functools

import jax
import jax.numpy as jnp
from jax import lax
from jax.experimental import pallas as pl
from jax.experimental.pallas import tpu as pltpu
from jax.sharding import PartitionSpec as P

SRC_DEV = 4096
SEG_DEV = 128
CAL = 524288
LANES = 128
LOW = 256
F32 = jnp.float32
BF16 = jnp.bfloat16
MESH = pl.DeviceIdType.MESH
UNROLL = 4

index_pairs = [(i, j) for i in range(5) for j in range(i, 5)]
NT = (((1,), (1,)), ((), ()))
NN = (((1,), (0,)), ((), ()))


def split(values):
    first = values.astype(BF16).astype(F32)
    return first, values - first


def one_hot(rows, index):
    grid = lax.broadcasted_iota(jnp.int32, (rows, index.shape[1]), 0)
    return jnp.where(grid == index, 1.0, 0.0).astype(BF16)


def solve_rows(entries):
    matrix = {}
    for position, (i, j) in enumerate(index_pairs):
        matrix[i, j] = entries[position] + (1.0 if i == j else 0.0)
    right_side = entries[15:20]
    factor = {}
    inverse = []
    for j in range(5):
        running = matrix[j, j]
        for k in range(j):
            running = running - factor[j, k] * factor[j, k]
        inverse.append(1.0 / jnp.sqrt(running))
        for i in range(j + 1, 5):
            running = matrix[j, i]
            for k in range(j):
                running = running - factor[i, k] * factor[j, k]
            factor[i, j] = running * inverse[j]
    forward = []
    for i in range(5):
        running = right_side[i]
        for k in range(i):
            running = running - factor[i, k] * forward[k]
        forward.append(running * inverse[i])
    result = [None] * 5
    for i in reversed(range(5)):
        running = forward[i]
        for k in range(i + 1, 5):
            running = running - factor[k, i] * result[k]
        result[i] = running * inverse[i]
    return result


def fold(total):
    return jnp.sum(total, axis=0, keepdims=True)


def fold_all(scratch, totals):
    count = len(totals)
    for q, total in enumerate(totals):
        scratch[q * 8 : q * 8 + 8, :] = total
    folded = scratch[pl.ds(0, count, stride=8), :]
    for s in range(1, 8):
        folded = folded + scratch[pl.ds(s, count, stride=8), :]
    return folded


def kernel(
    sizes,
    src_hbm,
    att_hbm,
    cal_hbm,
    phase_hbm,
    res_hbm,
    source_ref,
    segment_ref,
    unit_ref,
    live_ref,
    src_out,
    knot_out,
    unit_out,
    src_in,
    att_in,
    cal_in,
    phase_in,
    res_in,
    src_t,
    att_t,
    basis_t,
    cal_t,
    sums,
    knot_sums,
    unit_sums,
    low_hot,
    spread,
    table,
    fov_in,
    half,
    table_in,
    total_ref,
    folds_0,
    folds_1,
    folds_2,
    folds_3,
    update,
    chosen,
    rank_row,
    slot_hot,
    knot_send,
    knot_in,
    unit_send,
    unit_in,
    chunk_sems,
    whole_sems,
    fov_sems,
    table_sems,
    update_sems,
    knot_sems,
    unit_sems,
):
    n_sky, n_tm, n_fov = sizes
    devices = n_sky * n_tm * n_fov
    blocks = res_hbm.shape[0]
    steps = blocks // LANES // UNROLL
    folds = (folds_0, folds_1, folds_2, folds_3)
    parts = n_tm * n_fov
    high = SRC_DEV // LOW
    per_part = high // parts
    plane = n_sky * n_fov
    share = CAL // devices
    cuts = SRC_DEV // parts // LANES

    sky = lax.axis_index("sky")
    tm = lax.axis_index("tm")
    fov = lax.axis_index("fov")
    me = (sky * n_tm + tm) * n_fov + fov
    part_me = fov * n_tm + tm
    plane_me = sky * n_fov + fov

    def any_peer(k):
        q = lax.rem(me + k, devices)
        return (
            lax.div(q, n_tm * n_fov),
            lax.rem(lax.div(q, n_fov), n_tm),
            lax.rem(q, n_fov),
        )

    def chunk_copies(g):
        size = UNROLL * LANES
        rows = pl.ds(pl.multiple_of(g * size, size), size)
        return (
            pltpu.make_async_copy(src_hbm.at[:, rows], src_in.at[:, rows], chunk_sems.at[0, g]),
            pltpu.make_async_copy(res_hbm.at[rows], res_in.at[rows], chunk_sems.at[1, g]),
        )

    whole_copies = [
        pltpu.make_async_copy(att_hbm, att_in, whole_sems.at[0]),
        pltpu.make_async_copy(cal_hbm, cal_in, whole_sems.at[1]),
        pltpu.make_async_copy(phase_hbm, phase_in, whole_sems.at[2]),
    ]

    def start_chunk(g, carry):
        for copy in chunk_copies(g):
            copy.start()
        return carry

    lax.fori_loop(0, steps, start_chunk, 0)
    for copy in whole_copies:
        copy.start()

    barrier = pltpu.get_barrier_semaphore()
    for k in range(1, devices):
        pl.semaphore_signal(barrier, inc=1, device_id=any_peer(k), device_id_type=MESH)

    source = source_ref[...]
    source_high = source >> 8
    low_hot[...] = one_hot(LOW, source & (LOW - 1))

    def group_rows(g, u):
        return pl.ds(pl.multiple_of((g * UNROLL + u) * LANES, LANES), LANES)

    def source_sums(g, carry):
        for copy in chunk_copies(g):
            copy.wait()
        for u in range(UNROLL):
            rows = group_rows(g, u)
            for c in range(5):
                src_t[g, u, c] = src_in[c, rows, :].T
            src_t[g, u, 5] = res_in[rows, :].T
            totals = None
            for t in range(LANES // 8):
                tile = pl.ds(t * 8, 8)
                a = [src_t[g, u, c, tile, :] for c in range(6)]
                terms = [a[i] * a[j] for i, j in index_pairs] + [a[i] * a[5] for i in range(5)]
                totals = terms if totals is None else [x + y for x, y in zip(totals, terms)]
            sums[0:20, rows] = fold_all(folds[u], totals)
        return carry

    lax.fori_loop(0, steps, source_sums, 0)
    sums[20:24, :] = jnp.zeros((4, blocks), F32)

    live = lax.broadcasted_iota(jnp.int32, (1, blocks), 1) < live_ref[0]
    pair = jnp.concatenate(split(jnp.where(live, sums[...], 0.0)), axis=0)
    for h in range(high):
        spread[48 * h : 48 * h + 48, :] = jnp.where(source_high == h, pair, 0.0).astype(BF16)
    placed = lax.dot_general(
        spread[: 48 * high, :], low_hot[...], NT, preferred_element_type=F32
    )
    for h in range(high):
        piece = placed[48 * h : 48 * h + 24] + placed[48 * h + 24 : 48 * h + 48]
        p = h // per_part
        for l in range(LOW // LANES):
            row = ((h % per_part) * (LOW // LANES) + l) * 20
            table[p // n_tm, p % n_tm, row : row + 20, :] = piece[
                :20, l * LANES : (l + 1) * LANES
            ]

    pl.semaphore_wait(barrier, devices - 1)

    fov_copies = []
    for k in range(1, n_fov):
        f = lax.rem(fov + k, n_fov)
        copy = pltpu.make_async_remote_copy(
            src_ref=table.at[f],
            dst_ref=fov_in.at[k],
            send_sem=fov_sems.at[0, k],
            recv_sem=fov_sems.at[1, k],
            device_id=(sky, tm, f),
            device_id_type=MESH,
        )
        copy.start()
        fov_copies.append(copy)

    for copy in whole_copies:
        copy.wait()

    def fixed_sums(g, carry):
        for u in range(UNROLL):
            rows = group_rows(g, u)
            for c in range(4):
                att_t[g, u, c] = att_in[rows, c, :].T
            cal_t[g, u] = cal_in[rows, :].T
            phase_t = phase_in[rows, :].T
            rest = 1.0 - phase_t
            square = phase_t * phase_t
            cubed = square * phase_t
            basis_t[g, u, 0] = rest * rest * rest * (1.0 / 6.0)
            basis_t[g, u, 1] = (3.0 * cubed - 6.0 * square + 4.0) * (1.0 / 6.0)
            basis_t[g, u, 2] = (-3.0 * cubed + 3.0 * square + 3.0 * phase_t + 1.0) * (1.0 / 6.0)
            basis_t[g, u, 3] = cubed * (1.0 / 6.0)
            totals = None
            for t in range(LANES // 8):
                tile = pl.ds(t * 8, 8)
                b = [basis_t[g, u, j, tile, :] for j in range(4)]
                h = [att_t[g, u, c, tile, :] for c in range(4)]
                b = [x * x for x in b]
                h = [x * x for x in h]
                w = cal_t[g, u, tile, :]
                terms = [b[j] * h[c] for j in range(4) for c in range(4)] + [w * w]
                totals = terms if totals is None else [x + y for x, y in zip(totals, terms)]
            folded = fold_all(folds[u], totals)
            knot_sums[16:32, rows] = folded[0:16]
            unit_sums[1:2, rows] = folded[16:17]
        return carry

    lax.fori_loop(0, 1, fixed_sums, 0)

    for copy in fov_copies:
        copy.wait_recv()
    for t in range(n_tm):
        total = table[fov, t]
        for k in range(1, n_fov):
            total = total + fov_in[k, t]
        half[t] = total
    table_copies = []
    for k in range(1, n_tm):
        t = lax.rem(tm + k, n_tm)
        copy = pltpu.make_async_remote_copy(
            src_ref=half.at[t],
            dst_ref=table_in.at[k],
            send_sem=table_sems.at[0, k],
            recv_sem=table_sems.at[1, k],
            device_id=(sky, t, fov),
            device_id_type=MESH,
        )
        copy.start()
        table_copies.append(copy)

    lax.fori_loop(1, steps, fixed_sums, 0)

    for copy in table_copies:
        copy.wait_recv()
    total = half[tm]
    for k in range(1, n_tm):
        total = total + table_in[k]
    total_ref[...] = total
    solved = solve_rows([total_ref[pl.ds(q, cuts, stride=20), :] for q in range(20)])
    for c in range(5):
        update[part_me, c * cuts : (c + 1) * cuts, :] = solved[c]

    update_copies = []
    for k in range(1, parts):
        p = lax.rem(part_me + k, parts)
        copy = pltpu.make_async_remote_copy(
            src_ref=update.at[part_me],
            dst_ref=update.at[part_me],
            send_sem=update_sems.at[0, k],
            recv_sem=update_sems.at[1, k],
            device_id=(sky, lax.rem(p, n_tm), lax.div(p, n_tm)),
            device_id_type=MESH,
        )
        copy.start()
        update_copies.append(copy)

    unit = unit_ref[...]
    owner = lax.div(unit, share)
    local = unit - owner * share
    row = lax.broadcasted_iota(jnp.int32, (LANES, 2 * LANES), 0)
    column = lax.broadcasted_iota(jnp.int32, (LANES, 2 * LANES), 1)
    ramp = jnp.where(row <= column, 1.0, 0.0).astype(BF16)
    before = jnp.zeros((devices, LANES), F32)
    for g in range(blocks // LANES):
        cut = slice(g * LANES, (g + 1) * LANES)
        hot = lax.broadcasted_iota(jnp.int32, (devices, LANES), 0) == owner[:, cut]
        hot = jnp.where(hot, 1.0, 0.0)
        counts = lax.dot_general(hot.astype(BF16), ramp, NN, preferred_element_type=F32)
        rank_row[:, cut] = fold(hot * (counts[:, :LANES] + before)) - 1.0
        before = before + counts[:, LANES:]
    slot_hot[...] = one_hot(LANES, rank_row[...].astype(jnp.int32))

    for k in range(1, parts):
        p = lax.rem(part_me + parts - k, parts)
        pltpu.make_async_remote_copy(
            src_ref=update.at[part_me],
            dst_ref=update.at[p],
            send_sem=update_sems.at[0, k],
            recv_sem=update_sems.at[1, k],
            device_id=(sky, lax.rem(p, n_tm), lax.div(p, n_tm)),
            device_id_type=MESH,
        ).wait_recv()

    pieces = []
    for h in range(high):
        start = (h % per_part) * (LOW // LANES)
        piece = jnp.concatenate(
            [
                update[h // per_part, pl.ds(start + l, 5, stride=cuts), :]
                for l in range(LOW // LANES)
            ],
            axis=1,
        )
        src_out[:, h * LOW : (h + 1) * LOW] = piece
        pieces.extend(split(jnp.concatenate([piece, jnp.zeros((3, LOW), F32)], axis=0)))
    picked = lax.dot_general(
        jnp.concatenate(pieces, axis=0).astype(BF16),
        low_hot[...],
        NN,
        preferred_element_type=F32,
    )
    total = jnp.zeros((8, blocks), F32)
    for h in range(high):
        piece = picked[16 * h : 16 * h + 8] + picked[16 * h + 8 : 16 * h + 16]
        total = jnp.where(source_high == h, piece, total)
    chosen[...] = total

    def residual_sums(g, carry):
        for u in range(UNROLL):
            rows = group_rows(g, u)
            x = [jnp.broadcast_to(chosen[c : c + 1, rows], (8, LANES)) for c in range(5)]
            totals = None
            for t in range(LANES // 8):
                tile = pl.ds(t * 8, 8)
                taken = src_t[g, u, 0, tile, :] * x[0]
                for c in range(1, 5):
                    taken = taken + src_t[g, u, c, tile, :] * x[c]
                residual = src_t[g, u, 5, tile, :] - taken
                b = [basis_t[g, u, j, tile, :] for j in range(4)]
                h = [att_t[g, u, c, tile, :] * residual for c in range(4)]
                terms = [b[j] * h[c] for j in range(4) for c in range(4)]
                terms.append(cal_t[g, u, tile, :] * residual)
                totals = terms if totals is None else [y + z for y, z in zip(totals, terms)]
            folded = fold_all(folds[u], totals)
            knot_sums[0:16, rows] = folded[0:16]
            unit_sums[0:1, rows] = folded[16:17]
        return carry

    lax.fori_loop(0, steps, residual_sums, 0)

    unit_pair = jnp.where(live, unit_sums[0:2, :], 0.0)
    first, second = split(unit_pair)
    local_high = (local >> 7).astype(F32)
    local_low = (local & (LANES - 1)).astype(F32)
    fields = jnp.concatenate(
        [first, local_high, local_low, second, jnp.zeros((2, blocks), F32)], axis=0
    )
    for o in range(0, devices, 2):
        both = [jnp.where(owner == o + i, fields, 0.0) for i in range(2)]
        spread[8 * o : 8 * o + 16, :] = jnp.concatenate(both, axis=0).astype(BF16)
    packed = lax.dot_general(
        spread[: 8 * devices, :], slot_hot[...], NT, preferred_element_type=F32
    )
    for o in range(devices):
        unit_send[o] = packed[8 * o : 8 * o + 4] + packed[8 * o + 4 : 8 * o + 8]

    unit_copies = []
    for k in range(1, devices):
        copy = pltpu.make_async_remote_copy(
            src_ref=unit_send.at[lax.rem(me + k, devices)],
            dst_ref=unit_in.at[k],
            send_sem=unit_sems.at[0, k],
            recv_sem=unit_sems.at[1, k],
            device_id=any_peer(k),
            device_id_type=MESH,
        )
        copy.start()
        unit_copies.append(copy)

    segment = segment_ref[...]
    segment_high = segment >> 7
    segment_hot = one_hot(SEG_DEV, segment & (SEG_DEV - 1))
    pair = jnp.concatenate(split(jnp.where(live, knot_sums[...], 0.0)), axis=0)
    for h in range(n_sky):
        spread[64 * h : 64 * h + 64, :] = jnp.where(segment_high == h, pair, 0.0).astype(BF16)
    placed = lax.dot_general(
        spread[: 64 * n_sky, :], segment_hot, NT, preferred_element_type=F32
    )
    wide = jnp.concatenate(
        [placed[64 * h : 64 * h + 32] + placed[64 * h + 32 : 64 * h + 64] for h in range(n_sky)],
        axis=1,
    )
    position = lax.broadcasted_iota(jnp.int32, (8, wide.shape[1]), 1)
    knots = jnp.concatenate([wide[0:4], wide[16:20]], axis=0)
    for j in range(1, 4):
        moved = jnp.concatenate(
            [wide[4 * j : 4 * j + 4], wide[4 * j + 16 : 4 * j + 20]], axis=0
        )
        knots = knots + jnp.where(position >= j, pltpu.roll(moved, j, 1), 0.0)
    for h in range(n_sky):
        knot_send[h] = knots[:, h * SEG_DEV : (h + 1) * SEG_DEV]

    knot_copies = []
    for k in range(1, plane):
        q = lax.rem(plane_me + k, plane)
        peer_sky = lax.div(q, n_fov)
        copy = pltpu.make_async_remote_copy(
            src_ref=knot_send.at[peer_sky],
            dst_ref=knot_in.at[k],
            send_sem=knot_sems.at[0, k],
            recv_sem=knot_sems.at[1, k],
            device_id=(peer_sky, tm, lax.rem(q, n_fov)),
            device_id_type=MESH,
        )
        copy.start()
        knot_copies.append(copy)

    for copy in unit_copies:
        copy.wait_recv()
    unit_in[0] = unit_send[me]
    unit_out[...] = jnp.concatenate([unit_in[k] for k in range(devices)], axis=1)

    for copy in knot_copies:
        copy.wait_recv()
    total = knot_send[sky]
    for k in range(1, plane):
        total = total + knot_in[k]
    knot_out[...] = total

    for copy in fov_copies + table_copies + update_copies + unit_copies + knot_copies:
        copy.wait_send()


def finish(src_hbm, knot_hbm, unit_hbm, src_out, att_out, cal_out, knot_ref, unit_ref, sems):
    unit_copy = pltpu.make_async_copy(unit_hbm, unit_ref, sems.at[0])
    knot_copy = pltpu.make_async_copy(knot_hbm, knot_ref, sems.at[1])
    src_copy = pltpu.make_async_copy(src_hbm, src_out, sems.at[2])
    unit_copy.start()
    knot_copy.start()
    src_copy.start()
    unit_copy.wait()
    knot_copy.wait()
    att_out[...] = knot_ref[0:4] / (1.0 + knot_ref[4:8])
    n = cal_out.shape[0]
    first, second = split(unit_ref[0:2])
    flat_high = unit_ref[2:3].astype(jnp.int32)
    flat_low = unit_ref[3:4].astype(jnp.int32)
    high_hit = lax.broadcasted_iota(jnp.int32, (n, unit_ref.shape[1]), 0) == flat_high
    rows = [first[0:1], second[0:1], first[1:2], second[1:2]]
    spread_units = jnp.concatenate(
        [jnp.where(high_hit, value, 0.0).astype(BF16) for value in rows], axis=0
    )
    units = lax.dot_general(
        spread_units, one_hot(LANES, flat_low), NT, preferred_element_type=F32
    )
    cal_out[...] = (units[:n] + units[n : 2 * n]) / (
        1.0 + (units[2 * n : 3 * n] + units[3 * n :])
    )
    src_copy.wait()


def shards(sizes, src, att, cal, phase, res, source, segment, unit, live):
    n_sky, n_tm, n_fov = sizes
    devices = n_sky * n_tm * n_fov
    blocks = src.shape[0]
    steps = blocks // LANES // UNROLL
    parts = n_tm * n_fov
    plane = n_sky * n_fov
    high = SRC_DEV // LOW
    cuts = SRC_DEV // parts // LANES
    spread_rows = max(48 * high, 8 * devices, 64 * n_sky)
    anywhere = pl.BlockSpec(memory_space=pl.ANY)
    vmem = pl.BlockSpec(memory_space=pltpu.VMEM)
    smem = pl.BlockSpec(memory_space=pltpu.SMEM)
    dma = pltpu.SemaphoreType.DMA
    updates, knots, units = pl.pallas_call(
        functools.partial(kernel, sizes),
        out_shape=(
            jax.ShapeDtypeStruct((5, SRC_DEV), F32),
            jax.ShapeDtypeStruct((8, SEG_DEV), F32),
            jax.ShapeDtypeStruct((4, devices * LANES), F32),
        ),
        in_specs=[anywhere] * 5 + [vmem] * 3 + [smem],
        out_specs=(vmem, vmem, vmem),
        scratch_shapes=[
            pltpu.VMEM((src.shape[1], blocks, LANES), F32),
            pltpu.VMEM(att.shape, F32),
            pltpu.VMEM(cal.shape, F32),
            pltpu.VMEM(phase.shape, F32),
            pltpu.VMEM(res.shape, F32),
            pltpu.VMEM((steps, UNROLL, 6, LANES, LANES), F32),
            pltpu.VMEM((steps, UNROLL, 4, LANES, LANES), F32),
            pltpu.VMEM((steps, UNROLL, 4, LANES, LANES), F32),
            pltpu.VMEM((steps, UNROLL, LANES, LANES), F32),
            pltpu.VMEM((24, blocks), F32),
            pltpu.VMEM((32, blocks), F32),
            pltpu.VMEM((8, blocks), F32),
            pltpu.VMEM((LOW, blocks), BF16),
            pltpu.VMEM((spread_rows, blocks), BF16),
            pltpu.VMEM((n_fov, n_tm, 20 * cuts, LANES), F32),
            pltpu.VMEM((n_fov, n_tm, 20 * cuts, LANES), F32),
            pltpu.VMEM((n_tm, 20 * cuts, LANES), F32),
            pltpu.VMEM((n_tm, 20 * cuts, LANES), F32),
            pltpu.VMEM((20 * cuts, LANES), F32),
            pltpu.VMEM((160, LANES), F32),
            pltpu.VMEM((160, LANES), F32),
            pltpu.VMEM((160, LANES), F32),
            pltpu.VMEM((160, LANES), F32),
            pltpu.VMEM((parts, 5 * cuts, LANES), F32),
            pltpu.VMEM((8, blocks), F32),
            pltpu.VMEM((1, blocks), F32),
            pltpu.VMEM((LANES, blocks), BF16),
            pltpu.VMEM((n_sky, 8, SEG_DEV), F32),
            pltpu.VMEM((plane, 8, SEG_DEV), F32),
            pltpu.VMEM((devices, 4, LANES), F32),
            pltpu.VMEM((devices, 4, LANES), F32),
            dma((2, steps)),
            dma((3,)),
            dma((2, n_fov)),
            dma((2, n_tm)),
            dma((2, parts)),
            dma((2, plane)),
            dma((2, devices)),
        ],
        compiler_params=pltpu.CompilerParams(
            collective_id=0, has_side_effects=True, vmem_limit_bytes=58 * 1024 * 1024
        ),
    )(
        jnp.transpose(src, (1, 0, 2)),
        att,
        cal,
        phase,
        res,
        source.reshape(1, blocks),
        segment.reshape(1, blocks),
        unit.reshape(1, blocks),
        live,
    )
    src_update, att_update, cal_update = pl.pallas_call(
        finish,
        out_shape=(
            jax.ShapeDtypeStruct((5, SRC_DEV), F32),
            jax.ShapeDtypeStruct((4, SEG_DEV), F32),
            jax.ShapeDtypeStruct((CAL // devices // LANES, LANES), F32),
        ),
        in_specs=[anywhere] * 3,
        out_specs=(anywhere, vmem, vmem),
        scratch_shapes=[
            pltpu.VMEM(knots.shape, F32),
            pltpu.VMEM(units.shape, F32),
            dma((3,)),
        ],
        compiler_params=pltpu.CompilerParams(vmem_limit_bytes=58 * 1024 * 1024),
    )(updates, knots, units)
    return (
        src_update,
        att_update.reshape(4, 1, SEG_DEV),
        cal_update.reshape(CAL // devices),
    )


def solution(mesh):
    sizes = (mesh.shape["sky"], mesh.shape["tm"], mesh.shape["fov"])
    every = ("sky", "tm", "fov")
    return jax.shard_map(
        functools.partial(shards, sizes),
        mesh=mesh,
        in_specs=(
            P(every, None, None),
            P(every, None, None),
            P(every, None),
            P(every, None),
            P(every, None),
            P(every),
            P(every),
            P(every),
            P(every),
        ),
        out_specs=(P(None, "sky"), P(None, "tm", "sky"), P(every)),
        check_vma=False,
    )
```

```python
import functools

import jax
import jax.numpy as jnp
from jax import lax
from jax.experimental import pallas as pl
from jax.experimental.pallas import tpu as pltpu
from jax.sharding import PartitionSpec as P

SRC_DEV = 4096
SEG_DEV = 128
CAL = 524288
LANES = 128
LOW = 256
F32 = jnp.float32
BF16 = jnp.bfloat16
MESH = pl.DeviceIdType.MESH
UNROLL = 4

index_pairs = [(i, j) for i in range(5) for j in range(i, 5)]
NT = (((1,), (1,)), ((), ()))
NN = (((1,), (0,)), ((), ()))


def split(values):
    first = values.astype(BF16).astype(F32)
    return first, values - first


def one_hot(rows, index):
    grid = lax.broadcasted_iota(jnp.int32, (rows, index.shape[1]), 0)
    return jnp.where(grid == index, 1.0, 0.0).astype(BF16)


def solve_rows(entries):
    matrix = {}
    for position, (i, j) in enumerate(index_pairs):
        matrix[i, j] = entries[position] + (1.0 if i == j else 0.0)
    right_side = entries[15:20]
    factor = {}
    inverse = []
    for j in range(5):
        running = matrix[j, j]
        for k in range(j):
            running = running - factor[j, k] * factor[j, k]
        inverse.append(1.0 / jnp.sqrt(running))
        for i in range(j + 1, 5):
            running = matrix[j, i]
            for k in range(j):
                running = running - factor[i, k] * factor[j, k]
            factor[i, j] = running * inverse[j]
    forward = []
    for i in range(5):
        running = right_side[i]
        for k in range(i):
            running = running - factor[i, k] * forward[k]
        forward.append(running * inverse[i])
    result = [None] * 5
    for i in reversed(range(5)):
        running = forward[i]
        for k in range(i + 1, 5):
            running = running - factor[k, i] * result[k]
        result[i] = running * inverse[i]
    return result


def fold(total):
    return jnp.sum(total, axis=0, keepdims=True)


def fold_all(scratch, totals):
    count = len(totals)
    for q, total in enumerate(totals):
        scratch[q * 8 : q * 8 + 8, :] = total
    folded = scratch[pl.ds(0, count, stride=8), :]
    for s in range(1, 8):
        folded = folded + scratch[pl.ds(s, count, stride=8), :]
    return folded


def kernel(
    sizes,
    src_hbm,
    att_hbm,
    cal_hbm,
    phase_hbm,
    res_hbm,
    source_ref,
    segment_ref,
    unit_ref,
    live_ref,
    src_out,
    att_out,
    cal_out,
    src_in,
    att_in,
    cal_in,
    phase_in,
    res_in,
    src_t,
    att_t,
    basis_t,
    cal_t,
    sums,
    knot_sums,
    unit_sums,
    low_hot,
    spread,
    table,
    fov_in,
    half,
    table_in,
    total_ref,
    folds_0,
    folds_1,
    folds_2,
    folds_3,
    update,
    chosen,
    rank_row,
    slot_hot,
    knot_send,
    knot_in,
    early_send,
    early_in,
    unit_send,
    unit_in,
    flat_hot,
    chunk_sems,
    whole_sems,
    fov_sems,
    table_sems,
    update_sems,
    knot_sems,
    early_sems,
    unit_sems,
):
    n_sky, n_tm, n_fov = sizes
    devices = n_sky * n_tm * n_fov
    blocks = res_hbm.shape[0]
    steps = blocks // LANES // UNROLL
    folds = (folds_0, folds_1, folds_2, folds_3)
    parts = n_tm * n_fov
    high = SRC_DEV // LOW
    per_part = high // parts
    plane = n_sky * n_fov
    share = CAL // devices
    unit_high = share // LANES
    cuts = SRC_DEV // parts // LANES

    sky = lax.axis_index("sky")
    tm = lax.axis_index("tm")
    fov = lax.axis_index("fov")
    me = (sky * n_tm + tm) * n_fov + fov
    part_me = fov * n_tm + tm
    plane_me = sky * n_fov + fov

    def any_peer(k):
        q = lax.rem(me + k, devices)
        return (
            lax.div(q, n_tm * n_fov),
            lax.rem(lax.div(q, n_fov), n_tm),
            lax.rem(q, n_fov),
        )

    def chunk_copies(g):
        size = UNROLL * LANES
        rows = pl.ds(pl.multiple_of(g * size, size), size)
        return (
            pltpu.make_async_copy(src_hbm.at[:, rows], src_in.at[:, rows], chunk_sems.at[0, g]),
            pltpu.make_async_copy(res_hbm.at[rows], res_in.at[rows], chunk_sems.at[1, g]),
        )

    whole_copies = [
        pltpu.make_async_copy(att_hbm, att_in, whole_sems.at[0]),
        pltpu.make_async_copy(cal_hbm, cal_in, whole_sems.at[1]),
        pltpu.make_async_copy(phase_hbm, phase_in, whole_sems.at[2]),
    ]

    def start_chunk(g, carry):
        for copy in chunk_copies(g):
            copy.start()
        return carry

    lax.fori_loop(0, steps, start_chunk, 0)
    for copy in whole_copies:
        copy.start()

    barrier = pltpu.get_barrier_semaphore()
    for k in range(1, devices):
        pl.semaphore_signal(barrier, inc=1, device_id=any_peer(k), device_id_type=MESH)

    source = source_ref[...]
    source_high = source >> 8
    low_hot[...] = one_hot(LOW, source & (LOW - 1))

    def group_rows(g, u):
        return pl.ds(pl.multiple_of((g * UNROLL + u) * LANES, LANES), LANES)

    def source_sums(g, carry):
        for copy in chunk_copies(g):
            copy.wait()
        for u in range(UNROLL):
            rows = group_rows(g, u)
            for c in range(5):
                src_t[g, u, c] = src_in[c, rows, :].T
            src_t[g, u, 5] = res_in[rows, :].T
            totals = None
            for t in range(LANES // 8):
                tile = pl.ds(t * 8, 8)
                a = [src_t[g, u, c, tile, :] for c in range(6)]
                terms = [a[i] * a[j] for i, j in index_pairs] + [a[i] * a[5] for i in range(5)]
                totals = terms if totals is None else [x + y for x, y in zip(totals, terms)]
            sums[0:20, rows] = fold_all(folds[u], totals)
        return carry

    lax.fori_loop(0, steps, source_sums, 0)
    sums[20:24, :] = jnp.zeros((4, blocks), F32)

    live = lax.broadcasted_iota(jnp.int32, (1, blocks), 1) < live_ref[0]
    pair = jnp.concatenate(split(jnp.where(live, sums[...], 0.0)), axis=0)
    for h in range(high):
        spread[48 * h : 48 * h + 48, :] = jnp.where(source_high == h, pair, 0.0).astype(BF16)
    placed = lax.dot_general(
        spread[: 48 * high, :], low_hot[...], NT, preferred_element_type=F32
    )
    for h in range(high):
        piece = placed[48 * h : 48 * h + 24] + placed[48 * h + 24 : 48 * h + 48]
        p = h // per_part
        for l in range(LOW // LANES):
            row = ((h % per_part) * (LOW // LANES) + l) * 20
            table[p // n_tm, p % n_tm, row : row + 20, :] = piece[
                :20, l * LANES : (l + 1) * LANES
            ]

    pl.semaphore_wait(barrier, devices - 1)

    fov_copies = []
    for k in range(1, n_fov):
        f = lax.rem(fov + k, n_fov)
        copy = pltpu.make_async_remote_copy(
            src_ref=table.at[f],
            dst_ref=fov_in.at[k],
            send_sem=fov_sems.at[0, k],
            recv_sem=fov_sems.at[1, k],
            device_id=(sky, tm, f),
            device_id_type=MESH,
        )
        copy.start()
        fov_copies.append(copy)

    for copy in whole_copies:
        copy.wait()

    def fixed_sums(g, carry):
        for u in range(UNROLL):
            rows = group_rows(g, u)
            for c in range(4):
                att_t[g, u, c] = att_in[rows, c, :].T
            cal_t[g, u] = cal_in[rows, :].T
            phase_t = phase_in[rows, :].T
            rest = 1.0 - phase_t
            square = phase_t * phase_t
            cubed = square * phase_t
            basis_t[g, u, 0] = rest * rest * rest * (1.0 / 6.0)
            basis_t[g, u, 1] = (3.0 * cubed - 6.0 * square + 4.0) * (1.0 / 6.0)
            basis_t[g, u, 2] = (-3.0 * cubed + 3.0 * square + 3.0 * phase_t + 1.0) * (1.0 / 6.0)
            basis_t[g, u, 3] = cubed * (1.0 / 6.0)
            totals = None
            for t in range(LANES // 8):
                tile = pl.ds(t * 8, 8)
                b = [basis_t[g, u, j, tile, :] for j in range(4)]
                h = [att_t[g, u, c, tile, :] for c in range(4)]
                b = [x * x for x in b]
                h = [x * x for x in h]
                w = cal_t[g, u, tile, :]
                terms = [b[j] * h[c] for j in range(4) for c in range(4)] + [w * w]
                totals = terms if totals is None else [x + y for x, y in zip(totals, terms)]
            folded = fold_all(folds[u], totals)
            knot_sums[16:32, rows] = folded[0:16]
            unit_sums[1:2, rows] = folded[16:17]
        return carry

    lax.fori_loop(0, 1, fixed_sums, 0)

    for copy in fov_copies:
        copy.wait_recv()
    for t in range(n_tm):
        total = table[fov, t]
        for k in range(1, n_fov):
            total = total + fov_in[k, t]
        half[t] = total
    table_copies = []
    for k in range(1, n_tm):
        t = lax.rem(tm + k, n_tm)
        copy = pltpu.make_async_remote_copy(
            src_ref=half.at[t],
            dst_ref=table_in.at[k],
            send_sem=table_sems.at[0, k],
            recv_sem=table_sems.at[1, k],
            device_id=(sky, t, fov),
            device_id_type=MESH,
        )
        copy.start()
        table_copies.append(copy)

    lax.fori_loop(1, steps, fixed_sums, 0)

    for copy in table_copies:
        copy.wait_recv()
    total = half[tm]
    for k in range(1, n_tm):
        total = total + table_in[k]
    total_ref[...] = total
    solved = solve_rows([total_ref[pl.ds(q, cuts, stride=20), :] for q in range(20)])
    for c in range(5):
        update[part_me, c * cuts : (c + 1) * cuts, :] = solved[c]

    update_copies = []
    for k in range(1, parts):
        p = lax.rem(part_me + k, parts)
        copy = pltpu.make_async_remote_copy(
            src_ref=update.at[part_me],
            dst_ref=update.at[part_me],
            send_sem=update_sems.at[0, k],
            recv_sem=update_sems.at[1, k],
            device_id=(sky, lax.rem(p, n_tm), lax.div(p, n_tm)),
            device_id_type=MESH,
        )
        copy.start()
        update_copies.append(copy)

    unit = unit_ref[...]
    owner = lax.div(unit, share)
    local = unit - owner * share
    row = lax.broadcasted_iota(jnp.int32, (LANES, 2 * LANES), 0)
    column = lax.broadcasted_iota(jnp.int32, (LANES, 2 * LANES), 1)
    ramp = jnp.where(row <= column, 1.0, 0.0).astype(BF16)
    before = jnp.zeros((devices, LANES), F32)
    for g in range(blocks // LANES):
        cut = slice(g * LANES, (g + 1) * LANES)
        hot = lax.broadcasted_iota(jnp.int32, (devices, LANES), 0) == owner[:, cut]
        hot = jnp.where(hot, 1.0, 0.0)
        counts = lax.dot_general(hot.astype(BF16), ramp, NN, preferred_element_type=F32)
        rank_row[:, cut] = fold(hot * (counts[:, :LANES] + before)) - 1.0
        before = before + counts[:, LANES:]
    slot_hot[...] = one_hot(LANES, rank_row[...].astype(jnp.int32))

    owned = lax.broadcasted_iota(jnp.int32, (devices, blocks), 0) == owner

    def pack(rows):
        for q, value in enumerate(rows):
            spread[devices * q : devices * (q + 1), :] = jnp.where(owned, value, 0.0).astype(BF16)
        packed = lax.dot_general(
            spread[: devices * len(rows), :], slot_hot[...], NT, preferred_element_type=F32
        )
        return [packed[devices * q : devices * (q + 1)] for q in range(len(rows))]

    def send_units(source, target, sems):
        copies = []
        for k in range(1, devices):
            copy = pltpu.make_async_remote_copy(
                src_ref=source.at[lax.rem(me + k, devices)],
                dst_ref=target.at[k],
                send_sem=sems.at[0, k],
                recv_sem=sems.at[1, k],
                device_id=any_peer(k),
                device_id_type=MESH,
            )
            copy.start()
            copies.append(copy)
        return copies

    first, second = split(jnp.where(live, unit_sums[1:2, :], 0.0))
    local_high = (local >> 7).astype(F32)
    local_low = (local & (LANES - 1)).astype(F32)
    fields = pack([first, second, local_high, local_low])
    early_send[:, 0, :] = fields[0] + fields[1]
    early_send[:, 1, :] = fields[2]
    early_send[:, 2, :] = fields[3]
    early_send[:, 3, :] = jnp.zeros((devices, LANES), F32)
    early_copies = send_units(early_send, early_in, early_sems)

    for k in range(1, parts):
        p = lax.rem(part_me + parts - k, parts)
        pltpu.make_async_remote_copy(
            src_ref=update.at[part_me],
            dst_ref=update.at[p],
            send_sem=update_sems.at[0, k],
            recv_sem=update_sems.at[1, k],
            device_id=(sky, lax.rem(p, n_tm), lax.div(p, n_tm)),
            device_id_type=MESH,
        ).wait_recv()

    pieces = []
    for h in range(high):
        start = (h % per_part) * (LOW // LANES)
        piece = jnp.concatenate(
            [
                update[h // per_part, pl.ds(start + l, 5, stride=cuts), :]
                for l in range(LOW // LANES)
            ],
            axis=1,
        )
        src_out[:, h * LOW : (h + 1) * LOW] = piece
        pieces.extend(split(jnp.concatenate([piece, jnp.zeros((3, LOW), F32)], axis=0)))
    picked = lax.dot_general(
        jnp.concatenate(pieces, axis=0).astype(BF16),
        low_hot[...],
        NN,
        preferred_element_type=F32,
    )
    total = jnp.zeros((8, blocks), F32)
    for h in range(high):
        piece = picked[16 * h : 16 * h + 8] + picked[16 * h + 8 : 16 * h + 16]
        total = jnp.where(source_high == h, piece, total)
    chosen[...] = total

    def residual_sums(g, carry):
        for u in range(UNROLL):
            rows = group_rows(g, u)
            x = [jnp.broadcast_to(chosen[c : c + 1, rows], (8, LANES)) for c in range(5)]
            totals = None
            for t in range(LANES // 8):
                tile = pl.ds(t * 8, 8)
                taken = src_t[g, u, 0, tile, :] * x[0]
                for c in range(1, 5):
                    taken = taken + src_t[g, u, c, tile, :] * x[c]
                residual = src_t[g, u, 5, tile, :] - taken
                b = [basis_t[g, u, j, tile, :] for j in range(4)]
                h = [att_t[g, u, c, tile, :] * residual for c in range(4)]
                terms = [b[j] * h[c] for j in range(4) for c in range(4)]
                terms.append(cal_t[g, u, tile, :] * residual)
                totals = terms if totals is None else [y + z for y, z in zip(totals, terms)]
            folded = fold_all(folds[u], totals)
            knot_sums[0:16, rows] = folded[0:16]
            unit_sums[0:1, rows] = folded[16:17]
        return carry

    lax.fori_loop(0, steps, residual_sums, 0)

    fields = pack(split(jnp.where(live, unit_sums[0:1, :], 0.0)))
    unit_send[:, 0, :] = fields[0] + fields[1]
    unit_copies = send_units(unit_send, unit_in, unit_sems)

    segment = segment_ref[...]
    segment_high = segment >> 7
    segment_hot = one_hot(SEG_DEV, segment & (SEG_DEV - 1))
    pair = jnp.concatenate(split(jnp.where(live, knot_sums[...], 0.0)), axis=0)
    for h in range(n_sky):
        spread[64 * h : 64 * h + 64, :] = jnp.where(segment_high == h, pair, 0.0).astype(BF16)
    placed = lax.dot_general(
        spread[: 64 * n_sky, :], segment_hot, NT, preferred_element_type=F32
    )
    wide = jnp.concatenate(
        [placed[64 * h : 64 * h + 32] + placed[64 * h + 32 : 64 * h + 64] for h in range(n_sky)],
        axis=1,
    )
    position = lax.broadcasted_iota(jnp.int32, (8, wide.shape[1]), 1)
    knots = jnp.concatenate([wide[0:4], wide[16:20]], axis=0)
    for j in range(1, 4):
        moved = jnp.concatenate(
            [wide[4 * j : 4 * j + 4], wide[4 * j + 16 : 4 * j + 20]], axis=0
        )
        knots = knots + jnp.where(position >= j, pltpu.roll(moved, j, 1), 0.0)
    for h in range(n_sky):
        knot_send[h] = knots[:, h * SEG_DEV : (h + 1) * SEG_DEV]

    knot_copies = []
    for k in range(1, plane):
        q = lax.rem(plane_me + k, plane)
        peer_sky = lax.div(q, n_fov)
        copy = pltpu.make_async_remote_copy(
            src_ref=knot_send.at[peer_sky],
            dst_ref=knot_in.at[k],
            send_sem=knot_sems.at[0, k],
            recv_sem=knot_sems.at[1, k],
            device_id=(peer_sky, tm, lax.rem(q, n_fov)),
            device_id_type=MESH,
        )
        copy.start()
        knot_copies.append(copy)

    for copy in early_copies:
        copy.wait_recv()
    early_in[0] = early_send[me]
    flat = jnp.concatenate([early_in[k] for k in range(devices)], axis=1)
    flat_hot[...] = one_hot(LANES, flat[2:3].astype(jnp.int32))
    flat_high = flat[1:2].astype(jnp.int32)

    def place(value):
        hit = lax.broadcasted_iota(jnp.int32, (unit_high, value.shape[1]), 0) == flat_high
        halves = [jnp.where(hit, part, 0.0).astype(BF16) for part in split(value)]
        placed = lax.dot_general(
            jnp.concatenate(halves, axis=0), flat_hot[...], NT, preferred_element_type=F32
        )
        return placed[:unit_high] + placed[unit_high:]

    unit_diag = place(flat[0:1])

    for copy in knot_copies:
        copy.wait_recv()
    total = knot_send[sky]
    for k in range(1, plane):
        total = total + knot_in[k]
    att_out[...] = total[0:4] / (1.0 + total[4:8])

    for copy in unit_copies:
        copy.wait_recv()
    unit_in[0] = unit_send[me]
    unit_right = place(jnp.concatenate([unit_in[k] for k in range(devices)], axis=1))
    cal_out[...] = unit_right / (1.0 + unit_diag)

    for copy in fov_copies + table_copies + update_copies:
        copy.wait_send()
    for copy in early_copies + unit_copies + knot_copies:
        copy.wait_send()


def finish(*refs):
    count = (len(refs) - 1) // 2
    copies = [
        pltpu.make_async_copy(refs[i], refs[count + i], refs[-1].at[i]) for i in range(count)
    ]
    for copy in copies:
        copy.start()
    for copy in copies:
        copy.wait()


def shards(sizes, src, att, cal, phase, res, source, segment, unit, live):
    n_sky, n_tm, n_fov = sizes
    devices = n_sky * n_tm * n_fov
    blocks = src.shape[0]
    steps = blocks // LANES // UNROLL
    parts = n_tm * n_fov
    plane = n_sky * n_fov
    high = SRC_DEV // LOW
    cuts = SRC_DEV // parts // LANES
    spread_rows = max(48 * high, 8 * devices, 64 * n_sky)
    anywhere = pl.BlockSpec(memory_space=pl.ANY)
    vmem = pl.BlockSpec(memory_space=pltpu.VMEM)
    smem = pl.BlockSpec(memory_space=pltpu.SMEM)
    dma = pltpu.SemaphoreType.DMA
    out_shape = (
        jax.ShapeDtypeStruct((5, SRC_DEV), F32),
        jax.ShapeDtypeStruct((4, SEG_DEV), F32),
        jax.ShapeDtypeStruct((CAL // devices // LANES, LANES), F32),
    )
    results = pl.pallas_call(
        functools.partial(kernel, sizes),
        out_shape=out_shape,
        in_specs=[anywhere] * 5 + [vmem] * 3 + [smem],
        out_specs=(vmem, vmem, vmem),
        scratch_shapes=[
            pltpu.VMEM((src.shape[1], blocks, LANES), F32),
            pltpu.VMEM(att.shape, F32),
            pltpu.VMEM(cal.shape, F32),
            pltpu.VMEM(phase.shape, F32),
            pltpu.VMEM(res.shape, F32),
            pltpu.VMEM((steps, UNROLL, 6, LANES, LANES), F32),
            pltpu.VMEM((steps, UNROLL, 4, LANES, LANES), F32),
            pltpu.VMEM((steps, UNROLL, 4, LANES, LANES), F32),
            pltpu.VMEM((steps, UNROLL, LANES, LANES), F32),
            pltpu.VMEM((24, blocks), F32),
            pltpu.VMEM((32, blocks), F32),
            pltpu.VMEM((8, blocks), F32),
            pltpu.VMEM((LOW, blocks), BF16),
            pltpu.VMEM((spread_rows, blocks), BF16),
            pltpu.VMEM((n_fov, n_tm, 20 * cuts, LANES), F32),
            pltpu.VMEM((n_fov, n_tm, 20 * cuts, LANES), F32),
            pltpu.VMEM((n_tm, 20 * cuts, LANES), F32),
            pltpu.VMEM((n_tm, 20 * cuts, LANES), F32),
            pltpu.VMEM((20 * cuts, LANES), F32),
            pltpu.VMEM((160, LANES), F32),
            pltpu.VMEM((160, LANES), F32),
            pltpu.VMEM((160, LANES), F32),
            pltpu.VMEM((160, LANES), F32),
            pltpu.VMEM((parts, 5 * cuts, LANES), F32),
            pltpu.VMEM((8, blocks), F32),
            pltpu.VMEM((1, blocks), F32),
            pltpu.VMEM((LANES, blocks), BF16),
            pltpu.VMEM((n_sky, 8, SEG_DEV), F32),
            pltpu.VMEM((plane, 8, SEG_DEV), F32),
            pltpu.VMEM((devices, 4, LANES), F32),
            pltpu.VMEM((devices, 4, LANES), F32),
            pltpu.VMEM((devices, 1, LANES), F32),
            pltpu.VMEM((devices, 1, LANES), F32),
            pltpu.VMEM((LANES, devices * LANES), BF16),
            dma((2, steps)),
            dma((3,)),
            dma((2, n_fov)),
            dma((2, n_tm)),
            dma((2, parts)),
            dma((2, plane)),
            dma((2, devices)),
            dma((2, devices)),
        ],
        compiler_params=pltpu.CompilerParams(
            collective_id=0, has_side_effects=True, vmem_limit_bytes=58 * 1024 * 1024
        ),
    )(
        jnp.transpose(src, (1, 0, 2)),
        att,
        cal,
        phase,
        res,
        source.reshape(1, blocks),
        segment.reshape(1, blocks),
        unit.reshape(1, blocks),
        live,
    )
    src_update, att_update, cal_update = pl.pallas_call(
        finish,
        out_shape=out_shape,
        in_specs=[anywhere] * 3,
        out_specs=(vmem, vmem, vmem),
        scratch_shapes=[dma((3,))],
        compiler_params=pltpu.CompilerParams(vmem_limit_bytes=58 * 1024 * 1024),
    )(*results)
    return (
        src_update,
        att_update.reshape(4, 1, SEG_DEV),
        cal_update.reshape(CAL // devices),
    )


def solution(mesh):
    sizes = (mesh.shape["sky"], mesh.shape["tm"], mesh.shape["fov"])
    every = ("sky", "tm", "fov")
    return jax.shard_map(
        functools.partial(shards, sizes),
        mesh=mesh,
        in_specs=(
            P(every, None, None),
            P(every, None, None),
            P(every, None),
            P(every, None),
            P(every, None),
            P(every),
            P(every),
            P(every),
            P(every),
        ),
        out_specs=(P(None, "sky"), P(None, "tm", "sky"), P(every)),
        check_vma=False,
    )
```

```python
import functools

import jax
import jax.numpy as jnp
from jax import lax
from jax.experimental import pallas as pl
from jax.experimental.pallas import tpu as pltpu
from jax.sharding import PartitionSpec as P

SRC_DEV = 4096
SEG_DEV = 128
CAL = 524288
LANES = 128
LOW = 256
F32 = jnp.float32
BF16 = jnp.bfloat16
MESH = pl.DeviceIdType.MESH
UNROLL = 4

index_pairs = [(i, j) for i in range(5) for j in range(i, 5)]
NT = (((1,), (1,)), ((), ()))
NN = (((1,), (0,)), ((), ()))


def split(values):
    first = values.astype(BF16).astype(F32)
    return first, values - first


def one_hot(rows, index):
    grid = lax.broadcasted_iota(jnp.int32, (rows, index.shape[1]), 0)
    return jnp.where(grid == index, 1.0, 0.0).astype(BF16)


def solve_rows(entries):
    matrix = {}
    for position, (i, j) in enumerate(index_pairs):
        matrix[i, j] = entries[position] + (1.0 if i == j else 0.0)
    right_side = entries[15:20]
    factor = {}
    inverse = []
    for j in range(5):
        running = matrix[j, j]
        for k in range(j):
            running = running - factor[j, k] * factor[j, k]
        inverse.append(1.0 / jnp.sqrt(running))
        for i in range(j + 1, 5):
            running = matrix[j, i]
            for k in range(j):
                running = running - factor[i, k] * factor[j, k]
            factor[i, j] = running * inverse[j]
    forward = []
    for i in range(5):
        running = right_side[i]
        for k in range(i):
            running = running - factor[i, k] * forward[k]
        forward.append(running * inverse[i])
    result = [None] * 5
    for i in reversed(range(5)):
        running = forward[i]
        for k in range(i + 1, 5):
            running = running - factor[k, i] * result[k]
        result[i] = running * inverse[i]
    return result


def fold(total):
    return jnp.sum(total, axis=0, keepdims=True)


def fold_all(scratch, totals):
    count = len(totals)
    for q, total in enumerate(totals):
        scratch[q * 8 : q * 8 + 8, :] = total
    folded = scratch[pl.ds(0, count, stride=8), :]
    for s in range(1, 8):
        folded = folded + scratch[pl.ds(s, count, stride=8), :]
    return folded


def kernel(
    sizes,
    src_hbm,
    att_hbm,
    cal_hbm,
    phase_hbm,
    res_hbm,
    source_ref,
    segment_ref,
    unit_ref,
    live_ref,
    src_out,
    att_out,
    cal_out,
    src_in,
    att_in,
    cal_in,
    phase_in,
    res_in,
    src_t,
    att_t,
    basis_t,
    cal_t,
    sums,
    knot_sums,
    unit_sums,
    low_hot,
    spread,
    table,
    fov_in,
    half,
    table_in,
    total_ref,
    folds_0,
    folds_1,
    folds_2,
    folds_3,
    update,
    chosen,
    rank_row,
    slot_hot,
    knot_send,
    knot_in,
    early_send,
    early_in,
    unit_send,
    unit_in,
    flat_hot,
    chunk_sems,
    whole_sems,
    fov_sems,
    table_sems,
    update_sems,
    knot_sems,
    early_sems,
    unit_sems,
):
    n_sky, n_tm, n_fov = sizes
    devices = n_sky * n_tm * n_fov
    blocks = res_hbm.shape[0]
    steps = blocks // LANES // UNROLL
    folds = (folds_0, folds_1, folds_2, folds_3)
    parts = n_tm * n_fov
    high = SRC_DEV // LOW
    per_part = high // parts
    plane = n_sky * n_fov
    share = CAL // devices
    unit_high = share // LANES
    cuts = SRC_DEV // parts // LANES

    sky = lax.axis_index("sky")
    tm = lax.axis_index("tm")
    fov = lax.axis_index("fov")
    me = (sky * n_tm + tm) * n_fov + fov
    part_me = fov * n_tm + tm
    plane_me = sky * n_fov + fov

    def any_peer(k):
        q = lax.rem(me + k, devices)
        return (
            lax.div(q, n_tm * n_fov),
            lax.rem(lax.div(q, n_fov), n_tm),
            lax.rem(q, n_fov),
        )

    def chunk_copies(g):
        size = UNROLL * LANES
        rows = pl.ds(pl.multiple_of(g * size, size), size)
        return (
            pltpu.make_async_copy(src_hbm.at[:, rows], src_in.at[:, rows], chunk_sems.at[0, g]),
            pltpu.make_async_copy(res_hbm.at[rows], res_in.at[rows], chunk_sems.at[1, g]),
        )

    whole_copies = [
        pltpu.make_async_copy(att_hbm, att_in, whole_sems.at[0]),
        pltpu.make_async_copy(cal_hbm, cal_in, whole_sems.at[1]),
        pltpu.make_async_copy(phase_hbm, phase_in, whole_sems.at[2]),
    ]

    for g in range(min(2, steps)):
        for copy in chunk_copies(g):
            copy.start()

    barrier = pltpu.get_barrier_semaphore()
    for k in range(1, devices):
        pl.semaphore_signal(barrier, inc=1, device_id=any_peer(k), device_id_type=MESH)

    source = source_ref[...]
    source_high = source >> 8
    low_hot[...] = one_hot(LOW, source & (LOW - 1))

    def group_rows(g, u):
        return pl.ds(pl.multiple_of((g * UNROLL + u) * LANES, LANES), LANES)

    def wait_chunk(g):
        for copy in chunk_copies(g):
            copy.wait()

    def source_sums(g):
        for u in range(UNROLL):
            rows = group_rows(g, u)
            for c in range(5):
                src_t[g, u, c] = src_in[c, rows, :].T
            src_t[g, u, 5] = res_in[rows, :].T
            totals = None
            for t in range(LANES // 8):
                tile = pl.ds(t * 8, 8)
                a = [src_t[g, u, c, tile, :] for c in range(6)]
                terms = [a[i] * a[j] for i, j in index_pairs] + [a[i] * a[5] for i in range(5)]
                totals = terms if totals is None else [x + y for x, y in zip(totals, terms)]
            sums[0:20, rows] = fold_all(folds[u], totals)

    def first_steps(g, carry):
        wait_chunk(g)
        for copy in chunk_copies(g + 2):
            copy.start()
        source_sums(g)
        return carry

    def last_steps(g, carry):
        wait_chunk(g)
        source_sums(g)
        return carry

    lax.fori_loop(0, steps - 2, first_steps, 0)
    for copy in whole_copies:
        copy.start()
    lax.fori_loop(steps - 2, steps, last_steps, 0)

    live = lax.broadcasted_iota(jnp.int32, (1, blocks), 1) < live_ref[0]
    pair = jnp.concatenate(split(jnp.where(live, sums[...], 0.0)), axis=0)
    for h in range(0, high, 2):
        both = [jnp.where(source_high == h + i, pair, 0.0) for i in range(2)]
        spread[40 * h : 40 * h + 80, :] = jnp.concatenate(both, axis=0).astype(BF16)
    placed = lax.dot_general(
        spread[: 40 * high, :], low_hot[...], NT, preferred_element_type=F32
    )
    for h in range(high):
        piece = placed[40 * h : 40 * h + 20] + placed[40 * h + 20 : 40 * h + 40]
        p = h // per_part
        for l in range(LOW // LANES):
            row = ((h % per_part) * (LOW // LANES) + l) * 20
            table[p // n_tm, p % n_tm, row : row + 20, :] = piece[:, l * LANES : (l + 1) * LANES]

    pl.semaphore_wait(barrier, devices - 1)

    fov_copies = []
    for k in range(1, n_fov):
        f = lax.rem(fov + k, n_fov)
        copy = pltpu.make_async_remote_copy(
            src_ref=table.at[f],
            dst_ref=fov_in.at[k],
            send_sem=fov_sems.at[0, k],
            recv_sem=fov_sems.at[1, k],
            device_id=(sky, tm, f),
            device_id_type=MESH,
        )
        copy.start()
        fov_copies.append(copy)

    for copy in whole_copies:
        copy.wait()

    def fixed_sums(g, carry):
        for u in range(UNROLL):
            rows = group_rows(g, u)
            for c in range(4):
                att_t[g, u, c] = att_in[rows, c, :].T
            cal_t[g, u] = cal_in[rows, :].T
            phase_t = phase_in[rows, :].T
            rest = 1.0 - phase_t
            square = phase_t * phase_t
            cubed = square * phase_t
            basis_t[g, u, 0] = rest * rest * rest * (1.0 / 6.0)
            basis_t[g, u, 1] = (3.0 * cubed - 6.0 * square + 4.0) * (1.0 / 6.0)
            basis_t[g, u, 2] = (-3.0 * cubed + 3.0 * square + 3.0 * phase_t + 1.0) * (1.0 / 6.0)
            basis_t[g, u, 3] = cubed * (1.0 / 6.0)
            totals = None
            for t in range(LANES // 8):
                tile = pl.ds(t * 8, 8)
                b = [basis_t[g, u, j, tile, :] for j in range(4)]
                h = [att_t[g, u, c, tile, :] for c in range(4)]
                b = [x * x for x in b]
                h = [x * x for x in h]
                w = cal_t[g, u, tile, :]
                terms = [b[j] * h[c] for j in range(4) for c in range(4)] + [w * w]
                totals = terms if totals is None else [x + y for x, y in zip(totals, terms)]
            folded = fold_all(folds[u], totals)
            knot_sums[16:32, rows] = folded[0:16]
            unit_sums[1:2, rows] = folded[16:17]
        return carry

    lax.fori_loop(0, 1, fixed_sums, 0)

    for copy in fov_copies:
        copy.wait_recv()
    for t in range(n_tm):
        total = table[fov, t]
        for k in range(1, n_fov):
            total = total + fov_in[k, t]
        half[t] = total
    table_copies = []
    for k in range(1, n_tm):
        t = lax.rem(tm + k, n_tm)
        copy = pltpu.make_async_remote_copy(
            src_ref=half.at[t],
            dst_ref=table_in.at[k],
            send_sem=table_sems.at[0, k],
            recv_sem=table_sems.at[1, k],
            device_id=(sky, t, fov),
            device_id_type=MESH,
        )
        copy.start()
        table_copies.append(copy)

    lax.fori_loop(1, steps, fixed_sums, 0)

    for copy in table_copies:
        copy.wait_recv()
    total = half[tm]
    for k in range(1, n_tm):
        total = total + table_in[k]
    total_ref[...] = total
    solved = solve_rows([total_ref[pl.ds(q, cuts, stride=20), :] for q in range(20)])
    for c in range(5):
        update[part_me, c * cuts : (c + 1) * cuts, :] = solved[c]

    update_copies = []
    for k in range(1, parts):
        p = lax.rem(part_me + k, parts)
        copy = pltpu.make_async_remote_copy(
            src_ref=update.at[part_me],
            dst_ref=update.at[part_me],
            send_sem=update_sems.at[0, k],
            recv_sem=update_sems.at[1, k],
            device_id=(sky, lax.rem(p, n_tm), lax.div(p, n_tm)),
            device_id_type=MESH,
        )
        copy.start()
        update_copies.append(copy)

    unit = unit_ref[...]
    owner = lax.div(unit, share)
    local = unit - owner * share
    row = lax.broadcasted_iota(jnp.int32, (LANES, 2 * LANES), 0)
    column = lax.broadcasted_iota(jnp.int32, (LANES, 2 * LANES), 1)
    ramp = jnp.where(row <= column, 1.0, 0.0).astype(BF16)
    before = jnp.zeros((devices, LANES), F32)
    for g in range(blocks // LANES):
        cut = slice(g * LANES, (g + 1) * LANES)
        hot = lax.broadcasted_iota(jnp.int32, (devices, LANES), 0) == owner[:, cut]
        hot = jnp.where(hot, 1.0, 0.0)
        counts = lax.dot_general(hot.astype(BF16), ramp, NN, preferred_element_type=F32)
        rank_row[:, cut] = fold(hot * (counts[:, :LANES] + before)) - 1.0
        before = before + counts[:, LANES:]
    slot_hot[...] = one_hot(LANES, rank_row[...].astype(jnp.int32))

    owned = lax.broadcasted_iota(jnp.int32, (devices, blocks), 0) == owner

    def pack(rows):
        for q, value in enumerate(rows):
            spread[devices * q : devices * (q + 1), :] = jnp.where(owned, value, 0.0).astype(BF16)
        packed = lax.dot_general(
            spread[: devices * len(rows), :], slot_hot[...], NT, preferred_element_type=F32
        )
        return [packed[devices * q : devices * (q + 1)] for q in range(len(rows))]

    def send_units(source, target, sems):
        copies = []
        for k in range(1, devices):
            copy = pltpu.make_async_remote_copy(
                src_ref=source.at[lax.rem(me + k, devices)],
                dst_ref=target.at[k],
                send_sem=sems.at[0, k],
                recv_sem=sems.at[1, k],
                device_id=any_peer(k),
                device_id_type=MESH,
            )
            copy.start()
            copies.append(copy)
        return copies

    first, second = split(jnp.where(live, unit_sums[1:2, :], 0.0))
    local_high = (local >> 7).astype(F32)
    local_low = (local & (LANES - 1)).astype(F32)
    fields = pack([first, second, local_high, local_low])
    early_send[:, 0, :] = fields[0] + fields[1]
    early_send[:, 1, :] = fields[2]
    early_send[:, 2, :] = fields[3]
    early_send[:, 3, :] = jnp.zeros((devices, LANES), F32)
    early_copies = send_units(early_send, early_in, early_sems)

    for k in range(1, parts):
        p = lax.rem(part_me + parts - k, parts)
        pltpu.make_async_remote_copy(
            src_ref=update.at[part_me],
            dst_ref=update.at[p],
            send_sem=update_sems.at[0, k],
            recv_sem=update_sems.at[1, k],
            device_id=(sky, lax.rem(p, n_tm), lax.div(p, n_tm)),
            device_id_type=MESH,
        ).wait_recv()

    pieces = []
    for h in range(high):
        start = (h % per_part) * (LOW // LANES)
        piece = jnp.concatenate(
            [
                update[h // per_part, pl.ds(start + l, 5, stride=cuts), :]
                for l in range(LOW // LANES)
            ],
            axis=1,
        )
        src_out[:, h * LOW : (h + 1) * LOW] = piece
        pieces.extend(split(jnp.concatenate([piece, jnp.zeros((3, LOW), F32)], axis=0)))
    picked = lax.dot_general(
        jnp.concatenate(pieces, axis=0).astype(BF16),
        low_hot[...],
        NN,
        preferred_element_type=F32,
    )
    total = jnp.zeros((8, blocks), F32)
    for h in range(high):
        piece = picked[16 * h : 16 * h + 8] + picked[16 * h + 8 : 16 * h + 16]
        total = jnp.where(source_high == h, piece, total)
    chosen[...] = total

    def residual_sums(g, carry):
        for u in range(UNROLL):
            rows = group_rows(g, u)
            x = [jnp.broadcast_to(chosen[c : c + 1, rows], (8, LANES)) for c in range(5)]
            totals = None
            for t in range(LANES // 8):
                tile = pl.ds(t * 8, 8)
                taken = src_t[g, u, 0, tile, :] * x[0]
                for c in range(1, 5):
                    taken = taken + src_t[g, u, c, tile, :] * x[c]
                residual = src_t[g, u, 5, tile, :] - taken
                b = [basis_t[g, u, j, tile, :] for j in range(4)]
                h = [att_t[g, u, c, tile, :] * residual for c in range(4)]
                terms = [b[j] * h[c] for j in range(4) for c in range(4)]
                terms.append(cal_t[g, u, tile, :] * residual)
                totals = terms if totals is None else [y + z for y, z in zip(totals, terms)]
            folded = fold_all(folds[u], totals)
            knot_sums[0:16, rows] = folded[0:16]
            unit_sums[0:1, rows] = folded[16:17]
        return carry

    lax.fori_loop(0, steps, residual_sums, 0)

    fields = pack(split(jnp.where(live, unit_sums[0:1, :], 0.0)))
    unit_send[:, 0, :] = fields[0] + fields[1]
    unit_copies = send_units(unit_send, unit_in, unit_sems)

    segment = segment_ref[...]
    segment_high = segment >> 7
    segment_hot = one_hot(SEG_DEV, segment & (SEG_DEV - 1))
    pair = jnp.concatenate(split(jnp.where(live, knot_sums[...], 0.0)), axis=0)
    for h in range(n_sky):
        spread[64 * h : 64 * h + 64, :] = jnp.where(segment_high == h, pair, 0.0).astype(BF16)
    placed = lax.dot_general(
        spread[: 64 * n_sky, :], segment_hot, NT, preferred_element_type=F32
    )
    wide = jnp.concatenate(
        [placed[64 * h : 64 * h + 32] + placed[64 * h + 32 : 64 * h + 64] for h in range(n_sky)],
        axis=1,
    )
    position = lax.broadcasted_iota(jnp.int32, (8, wide.shape[1]), 1)
    knots = jnp.concatenate([wide[0:4], wide[16:20]], axis=0)
    for j in range(1, 4):
        moved = jnp.concatenate(
            [wide[4 * j : 4 * j + 4], wide[4 * j + 16 : 4 * j + 20]], axis=0
        )
        knots = knots + jnp.where(position >= j, pltpu.roll(moved, j, 1), 0.0)
    for h in range(n_sky):
        knot_send[h] = knots[:, h * SEG_DEV : (h + 1) * SEG_DEV]

    knot_copies = []
    for k in range(1, plane):
        q = lax.rem(plane_me + k, plane)
        peer_sky = lax.div(q, n_fov)
        copy = pltpu.make_async_remote_copy(
            src_ref=knot_send.at[peer_sky],
            dst_ref=knot_in.at[k],
            send_sem=knot_sems.at[0, k],
            recv_sem=knot_sems.at[1, k],
            device_id=(peer_sky, tm, lax.rem(q, n_fov)),
            device_id_type=MESH,
        )
        copy.start()
        knot_copies.append(copy)

    for copy in early_copies:
        copy.wait_recv()
    early_in[0] = early_send[me]
    flat = jnp.concatenate([early_in[k] for k in range(devices)], axis=1)
    flat_hot[...] = one_hot(LANES, flat[2:3].astype(jnp.int32))
    flat_high = flat[1:2].astype(jnp.int32)

    def place(value):
        hit = lax.broadcasted_iota(jnp.int32, (unit_high, value.shape[1]), 0) == flat_high
        halves = [jnp.where(hit, part, 0.0).astype(BF16) for part in split(value)]
        placed = lax.dot_general(
            jnp.concatenate(halves, axis=0), flat_hot[...], NT, preferred_element_type=F32
        )
        return placed[:unit_high] + placed[unit_high:]

    unit_diag = place(flat[0:1])

    for copy in knot_copies:
        copy.wait_recv()
    total = knot_send[sky]
    for k in range(1, plane):
        total = total + knot_in[k]
    att_out[...] = total[0:4] / (1.0 + total[4:8])

    for copy in unit_copies:
        copy.wait_recv()
    unit_in[0] = unit_send[me]
    unit_right = place(jnp.concatenate([unit_in[k] for k in range(devices)], axis=1))
    cal_out[...] = unit_right / (1.0 + unit_diag)

    for copy in fov_copies + table_copies + update_copies:
        copy.wait_send()
    for copy in early_copies + unit_copies + knot_copies:
        copy.wait_send()


def finish(*refs):
    count = (len(refs) - 1) // 2
    copies = [
        pltpu.make_async_copy(refs[i], refs[count + i], refs[-1].at[i]) for i in range(count)
    ]
    for copy in copies:
        copy.start()
    for copy in copies:
        copy.wait()


def shards(sizes, src, att, cal, phase, res, source, segment, unit, live):
    n_sky, n_tm, n_fov = sizes
    devices = n_sky * n_tm * n_fov
    blocks = src.shape[0]
    steps = blocks // LANES // UNROLL
    parts = n_tm * n_fov
    plane = n_sky * n_fov
    high = SRC_DEV // LOW
    cuts = SRC_DEV // parts // LANES
    spread_rows = max(40 * high, 8 * devices, 64 * n_sky)
    anywhere = pl.BlockSpec(memory_space=pl.ANY)
    vmem = pl.BlockSpec(memory_space=pltpu.VMEM)
    smem = pl.BlockSpec(memory_space=pltpu.SMEM)
    dma = pltpu.SemaphoreType.DMA
    out_shape = (
        jax.ShapeDtypeStruct((5, SRC_DEV), F32),
        jax.ShapeDtypeStruct((4, SEG_DEV), F32),
        jax.ShapeDtypeStruct((CAL // devices // LANES, LANES), F32),
    )
    results = pl.pallas_call(
        functools.partial(kernel, sizes),
        out_shape=out_shape,
        in_specs=[anywhere] * 5 + [vmem] * 3 + [smem],
        out_specs=(vmem, vmem, vmem),
        scratch_shapes=[
            pltpu.VMEM((src.shape[1], blocks, LANES), F32),
            pltpu.VMEM(att.shape, F32),
            pltpu.VMEM(cal.shape, F32),
            pltpu.VMEM(phase.shape, F32),
            pltpu.VMEM(res.shape, F32),
            pltpu.VMEM((steps, UNROLL, 6, LANES, LANES), F32),
            pltpu.VMEM((steps, UNROLL, 4, LANES, LANES), F32),
            pltpu.VMEM((steps, UNROLL, 4, LANES, LANES), F32),
            pltpu.VMEM((steps, UNROLL, LANES, LANES), F32),
            pltpu.VMEM((20, blocks), F32),
            pltpu.VMEM((32, blocks), F32),
            pltpu.VMEM((8, blocks), F32),
            pltpu.VMEM((LOW, blocks), BF16),
            pltpu.VMEM((spread_rows, blocks), BF16),
            pltpu.VMEM((n_fov, n_tm, 20 * cuts, LANES), F32),
            pltpu.VMEM((n_fov, n_tm, 20 * cuts, LANES), F32),
            pltpu.VMEM((n_tm, 20 * cuts, LANES), F32),
            pltpu.VMEM((n_tm, 20 * cuts, LANES), F32),
            pltpu.VMEM((20 * cuts, LANES), F32),
            pltpu.VMEM((160, LANES), F32),
            pltpu.VMEM((160, LANES), F32),
            pltpu.VMEM((160, LANES), F32),
            pltpu.VMEM((160, LANES), F32),
            pltpu.VMEM((parts, 5 * cuts, LANES), F32),
            pltpu.VMEM((8, blocks), F32),
            pltpu.VMEM((1, blocks), F32),
            pltpu.VMEM((LANES, blocks), BF16),
            pltpu.VMEM((n_sky, 8, SEG_DEV), F32),
            pltpu.VMEM((plane, 8, SEG_DEV), F32),
            pltpu.VMEM((devices, 4, LANES), F32),
            pltpu.VMEM((devices, 4, LANES), F32),
            pltpu.VMEM((devices, 1, LANES), F32),
            pltpu.VMEM((devices, 1, LANES), F32),
            pltpu.VMEM((LANES, devices * LANES), BF16),
            dma((2, steps)),
            dma((3,)),
            dma((2, n_fov)),
            dma((2, n_tm)),
            dma((2, parts)),
            dma((2, plane)),
            dma((2, devices)),
            dma((2, devices)),
        ],
        compiler_params=pltpu.CompilerParams(
            collective_id=0, has_side_effects=True, vmem_limit_bytes=58 * 1024 * 1024
        ),
    )(
        jnp.transpose(src, (1, 0, 2)),
        att,
        cal,
        phase,
        res,
        source.reshape(1, blocks),
        segment.reshape(1, blocks),
        unit.reshape(1, blocks),
        live,
    )
    src_update, att_update, cal_update = pl.pallas_call(
        finish,
        out_shape=out_shape,
        in_specs=[anywhere] * 3,
        out_specs=(vmem, vmem, vmem),
        scratch_shapes=[dma((3,))],
        compiler_params=pltpu.CompilerParams(vmem_limit_bytes=58 * 1024 * 1024),
    )(*results)
    return (
        src_update,
        att_update.reshape(4, 1, SEG_DEV),
        cal_update.reshape(CAL // devices),
    )


def solution(mesh):
    sizes = (mesh.shape["sky"], mesh.shape["tm"], mesh.shape["fov"])
    every = ("sky", "tm", "fov")
    return jax.shard_map(
        functools.partial(shards, sizes),
        mesh=mesh,
        in_specs=(
            P(every, None, None),
            P(every, None, None),
            P(every, None),
            P(every, None),
            P(every, None),
            P(every),
            P(every),
            P(every),
            P(every),
        ),
        out_specs=(P(None, "sky"), P(None, "tm", "sky"), P(every)),
        check_vma=False,
    )
```
